32 devices in a mesh: row: 4 (over x, core), col: 8 (over z, y).
Axes of the slice: x: 2, y: 2, z: 4, core: 2. Of those that a mesh axis runs over, the one named last changes fastest.
Arguments:
- inverse_first: float32 [6144, 6144], P('col', 'row'), as said below
- inverse_second: float32 [5120, 5120], P('col', 'row'), as said below
- inverse_third: float32 [4096, 4096], P('col', 'row'), as said below
- inverse_fourth: float32 [3072, 3072], P('col', 'row'), as said below
- coupling_first: float32 [1024, 6144], P('row', 'col'), may hold values from -0.078125 to 0.078125
- coupling_second: float32 [1024, 5120], P('row', 'col'), may hold values from -0.078125 to 0.078125
- coupling_third: float32 [1024, 4096], P('row', 'col'), may hold values from -0.09375 to 0.09375
- coupling_fourth: float32 [1024, 3072], P('row', 'col'), may hold values from -0.109375 to 0.109375
- inverse_root: float32 [16384, 16384], P('col', 'row'), as said below
- loads_first: float32 [6144, 512], P('row'), may hold values from -6 to 6
- loads_second: float32 [5120, 512], P('row'), may hold values from -6 to 6
- loads_third: float32 [4096, 512], P('row'), may hold values from -6 to 6
- loads_fourth: float32 [3072, 512], P('row'), may hold values from -6 to 6
- loads_root: float32 [16384, 512], P('row'), may hold values from -6 to 6
- target_blocks: int32 [4, 8], replicated, may hold values from 0 to 127, as said below
Outputs:
- solved_first: float32 [6144, 512], P(('row', 'col'))
- solved_second: float32 [5120, 512], P(('row', 'col'))
- solved_third: float32 [4096, 512], P(('row', 'col'))
- solved_fourth: float32 [3072, 512], P(('row', 'col'))
- solved_root: float32 [16384, 512], P('col')
The draws below stay inside these ranges and needn't reach their ends.
Inputs may be any that keep to these rules, and one draw needn't show every extreme that they name: `target_blocks`: within each row the entries are distinct; entry [k, j] is the root block of 128 rows that receives block j of the k-th child's coupling rows. Different children may share root blocks. `inverse_first`: lower triangular with a positive diagonal. `inverse_second`: lower triangular with a positive diagonal. `inverse_third`: lower triangular with a positive diagonal. `inverse_fourth`: lower triangular with a positive diagonal. `inverse_root`: Symmetric.
All inputs are finite; a program needn't handle non-finite values.
Results may differ from the reference program's by a relative error of at most 0.0001.
Values sent between devices are 32-bit elements; how exact they have to be, the bound alone decides.
No kernel may reach another device: no remote copies, remote signals or barrier semaphores. Data moves between devices by JAX's collectives and lax.ppermute only.
A program may use at most 192 MiB of HBM per device.

```python
import jax
import jax.numpy as jnp
from jax import lax

N1 = 6144
N2 = 5120
N3 = 4096
N4 = 3072
ROOT = 16384
COUPLE = 1024
BLOCK = 128
RHS = 512


def lower_inverse(base_key, order):
    first_key, second_key = jax.random.split(base_key)
    spread = jnp.clip(jax.random.normal(first_key, (order, order), jnp.float32), -6.0, 6.0)
    lower = jnp.tril(spread, -1) / jnp.sqrt(jnp.float32(order))
    diagonal = jnp.exp(jax.random.uniform(second_key, (order,), jnp.float32, -0.6931472, 0.6931472))
    return lower + jnp.diag(diagonal)


def draw_inverse_first(key, part):
    return lower_inverse(jax.random.fold_in(key, 101), N1)


def draw_inverse_second(key, part):
    return lower_inverse(jax.random.fold_in(key, 102), N2)


def draw_inverse_third(key, part):
    return lower_inverse(jax.random.fold_in(key, 103), N3)


def draw_inverse_fourth(key, part):
    return lower_inverse(jax.random.fold_in(key, 104), N4)


def draw_inverse_root(key, part):
    first_key, second_key = jax.random.split(jax.random.fold_in(key, 105))
    spread = jnp.clip(jax.random.normal(first_key, (ROOT, ROOT), jnp.float32), -6.0, 6.0)
    symmetric = (spread + spread.T) * (0.5 / jnp.sqrt(jnp.float32(ROOT)))
    diagonal = jax.random.uniform(second_key, (ROOT,), jnp.float32, 2.0, 3.0)
    return symmetric + jnp.diag(diagonal)


def draw_target_blocks(key, part):
    total = ROOT // BLOCK
    count = COUPLE // BLOCK
    listed = []
    for child in range(4):
        child_key = jax.random.fold_in(key, 211 + child)
        if child == 0:
            inner = jax.random.permutation(child_key, total - 2)[:count - 2].astype(jnp.int32) + 1
            ends = jnp.array([0, total - 1], jnp.int32)
            chosen = jnp.concatenate([ends, inner])
            order = jax.random.permutation(jax.random.fold_in(child_key, 5), count)
            listed.append(chosen[order])
        else:
            listed.append(jax.random.permutation(child_key, total)[:count].astype(jnp.int32))
    return jnp.stack(listed).astype(jnp.int32)


def level_of(own_key, extent, cuts, least, high):
    gain = 1.0
    for dim, blocks in cuts:
        steps = jax.random.uniform(jax.random.fold_in(jax.random.fold_in(own_key, 6), dim), (blocks,), jnp.float32, least / len(cuts), high / len(cuts))
        gain = gain * jnp.repeat(jnp.exp(steps), extent[dim] // blocks).reshape((-1,) + (1,) * (len(extent) - 1 - dim))
    return gain


def bell_draw(key, extent, scale, most, cuts=(), kind=jnp.bfloat16):
    gain = level_of(key, extent, cuts, -0.22, 0.18) if cuts else 1.0
    values = jax.random.normal(key, extent, jnp.float32) * scale * gain
    return jnp.minimum(jnp.maximum(values, -most), most).astype(kind)


def setup_inputs(seed: int = 0) -> dict:
    seeds = jax.random.split(jax.random.key(seed), 16)
    inverse_first = draw_inverse_first(jax.random.fold_in(seeds[15], 71), 0)
    inverse_second = draw_inverse_second(jax.random.fold_in(seeds[15], 71), 0)
    inverse_third = draw_inverse_third(jax.random.fold_in(seeds[15], 71), 0)
    inverse_fourth = draw_inverse_fourth(jax.random.fold_in(seeds[15], 71), 0)
    coupling_first = bell_draw(seeds[4], (COUPLE, N1), N1 ** -0.5, 0.078125, ((0, 4), (1, 8)), jnp.float32)
    coupling_second = bell_draw(seeds[5], (COUPLE, N2), N2 ** -0.5, 0.078125, ((0, 4), (1, 8)), jnp.float32)
    coupling_third = bell_draw(seeds[6], (COUPLE, N3), N3 ** -0.5, 0.09375, ((0, 4), (1, 8)), jnp.float32)
    coupling_fourth = bell_draw(seeds[7], (COUPLE, N4), N4 ** -0.5, 0.109375, ((0, 4), (1, 8)), jnp.float32)
    inverse_root = draw_inverse_root(jax.random.fold_in(seeds[15], 71), 0)
    loads_first = bell_draw(seeds[9], (N1, RHS), 1.0, 6.0, ((0, 4),), jnp.float32)
    loads_second = bell_draw(seeds[10], (N2, RHS), 1.0, 6.0, ((0, 4),), jnp.float32)
    loads_third = bell_draw(seeds[11], (N3, RHS), 1.0, 6.0, ((0, 4),), jnp.float32)
    loads_fourth = bell_draw(seeds[12], (N4, RHS), 1.0, 6.0, ((0, 4),), jnp.float32)
    loads_root = bell_draw(seeds[13], (ROOT, RHS), 1.0, 6.0, ((0, 4),), jnp.float32)
    target_blocks = draw_target_blocks(jax.random.fold_in(seeds[15], 71), 0)
    return dict(inverse_first=inverse_first, inverse_second=inverse_second, inverse_third=inverse_third, inverse_fourth=inverse_fourth, coupling_first=coupling_first, coupling_second=coupling_second, coupling_third=coupling_third, coupling_fourth=coupling_fourth, inverse_root=inverse_root, loads_first=loads_first, loads_second=loads_second, loads_third=loads_third, loads_fourth=loads_fourth, loads_root=loads_root, target_blocks=target_blocks)


def product(matrix, vector):
    return jnp.dot(matrix, vector, precision=lax.Precision.HIGHEST, preferred_element_type=jnp.float32)


def reference(inverse_first, inverse_second, inverse_third, inverse_fourth, coupling_first, coupling_second, coupling_third, coupling_fourth, inverse_root, loads_first, loads_second, loads_third, loads_fourth, loads_root, target_blocks):
    inverses = [inverse_first, inverse_second, inverse_third, inverse_fourth]
    couplings = [coupling_first, coupling_second, coupling_third, coupling_fourth]
    sources = [loads_first, loads_second, loads_third, loads_fourth]
    forward = [product(weight, source) for weight, source in zip(inverses, sources)]
    block_total = ROOT // BLOCK
    update = jnp.zeros((block_total, BLOCK, RHS), jnp.float32)
    for child in range(4):
        contribution = product(couplings[child], forward[child]).reshape(COUPLE // BLOCK, BLOCK, RHS)
        update = update.at[target_blocks[child]].add(contribution)
    shifted = loads_root - update.reshape(ROOT, RHS)
    solved_root = product(inverse_root, shifted)
    root_blocks = solved_root.reshape(block_total, BLOCK, RHS)
    results = []
    for child in range(4):
        picked = root_blocks[target_blocks[child]].reshape(COUPLE, RHS)
        reduced = forward[child] - product(couplings[child].T, picked)
        results.append(product(inverses[child].T, reduced))
    return (results[0], results[1], results[2], results[3], solved_root)
```

```python
import jax
import jax.numpy as jnp
from jax import lax
from jax.experimental import pallas as pl
from jax.experimental.pallas import tpu as pltpu
from jax.sharding import PartitionSpec as P

BLOCK = 128
AXES = ("row", "col")
PARTS = 2


def product(matrix, vector):
    return jnp.dot(
        matrix, vector, precision=lax.Precision.HIGH, preferred_element_type=jnp.float32
    )


def transposed(matrix, vector):
    return lax.dot_general(
        matrix,
        vector,
        (((0,), (0,)), ((), ())),
        precision=lax.Precision.HIGH,
        preferred_element_type=jnp.float32,
    )


def pick(array, index, axis):
    return lax.dynamic_index_in_dim(array, index, axis, keepdims=False)


class Group:
    def __init__(self, rows, cols, axis, stride, size):
        self.size = size
        self.place = lax.rem(lax.axis_index(axis) // stride, size)
        self.pairs = []
        for step in range(1, size):
            listed = []
            for r in range(rows):
                for c in range(cols):
                    old = r if axis == "row" else c
                    digit = old // stride % size
                    new = old + ((digit + step) % size - digit) * stride
                    there = (new, c) if axis == "row" else (r, new)
                    listed.append((r * cols + c, there[0] * cols + there[1]))
            self.pairs.append(listed)

    def scatter_sum(self, array, axis):
        total = pick(array, self.place, axis)
        for step in range(1, self.size):
            sent = pick(array, lax.rem(self.place + step, self.size), axis)
            total = total + lax.ppermute(sent, AXES, self.pairs[step - 1])
        return total

    def gather(self, array, axis):
        if self.size == 1:
            return jnp.expand_dims(array, axis)
        held = [array]
        for step in range(1, self.size):
            held.append(lax.ppermute(array, AXES, self.pairs[step - 1]))
        if self.size == 2:
            first = self.place == 0
            return jnp.stack(
                [jnp.where(first, held[0], held[1]), jnp.where(first, held[1], held[0])], axis
            )
        shape = array.shape[:axis] + (self.size,) + array.shape[axis:]
        out = jnp.zeros(shape, array.dtype)
        for step, value in enumerate(held):
            source = lax.rem(self.place + self.size - step, self.size)
            out = lax.dynamic_update_index_in_dim(out, value, source, axis)
        return out

    def total(self, array):
        if self.size == 2:
            return array + lax.ppermute(array, AXES, self.pairs[0])
        if self.size == 1:
            return array
        pieces = array.reshape((self.size, array.shape[0] // self.size) + array.shape[1:])
        return self.gather(self.scatter_sum(pieces, 0), 0).reshape(array.shape)


class Links:
    def __init__(self, rows, cols):
        cores = 2 if rows % 2 == 0 else 1
        near = 1
        while cols % (near * 2) == 0 and near * near * 8 <= cols * 2:
            near *= 2
        self.core = Group(rows, cols, "row", 1, cores)
        self.x = Group(rows, cols, "row", cores, rows // cores)
        self.y = Group(rows, cols, "col", 1, near)
        self.z = Group(rows, cols, "col", near, cols // near)

    def row_total(self, array):
        pieces = array.reshape((self.core.size, array.shape[0] // self.core.size, array.shape[1]))
        part = self.x.total(self.core.scatter_sum(pieces, 0))
        return self.core.gather(part, 0).reshape(array.shape)

    def col_scatter(self, array):
        size = array.shape[0] // (self.z.size * self.y.size)
        pieces = array.reshape(self.z.size, self.y.size, size, array.shape[1])
        return self.z.scatter_sum(self.y.scatter_sum(pieces, 1), 0)

    def col_gather(self, array):
        whole = self.y.gather(self.z.gather(array, 0), 1)
        return whole.reshape(-1, array.shape[-1])


def place_kernel(count, map_ref, loads_ref, blocks_ref, out_ref):
    here = pl.program_id(0)
    out_ref[...] = loads_ref[...]
    for child in range(map_ref.shape[0]):
        source = map_ref[child, here]

        @pl.when(source < count)
        def _():
            out_ref[...] -= blocks_ref[child, source]


def place(loads, blocks, slots, part, parts):
    children, count, size, width = blocks.shape
    owned = slots.shape[1]
    return pl.pallas_call(
        lambda *refs: place_kernel(count, *refs),
        grid_spec=pltpu.PrefetchScalarGridSpec(
            num_scalar_prefetch=1,
            grid=(owned,),
            in_specs=[
                pl.BlockSpec((size, width), lambda i, slots: (i, part)),
                pl.BlockSpec((children, count, size, width), lambda i, slots: (0, 0, 0, 0)),
            ],
            out_specs=pl.BlockSpec((size, width), lambda i, slots: (i, 0)),
        ),
        out_shape=jax.ShapeDtypeStruct((owned * size, width), jnp.float32),
        compiler_params=pltpu.CompilerParams(vmem_limit_bytes=40 * 2**20),
    )(slots, loads, blocks)


def take_kernel(count, ids_ref, held_ref, out_ref):
    source = ids_ref[pl.program_id(0)]
    inside = jnp.logical_and(source >= 0, source < count)

    @pl.when(inside)
    def _():
        out_ref[...] = held_ref[...]

    @pl.when(jnp.logical_not(inside))
    def _():
        out_ref[...] = jnp.zeros_like(out_ref)


def take(held, ids):
    rows, width = held.shape
    count = rows // BLOCK
    wanted = ids.shape[0]
    return pl.pallas_call(
        lambda *refs: take_kernel(count, *refs),
        grid_spec=pltpu.PrefetchScalarGridSpec(
            num_scalar_prefetch=1,
            grid=(wanted,),
            in_specs=[
                pl.BlockSpec(
                    (BLOCK, width), lambda i, ids: (jnp.clip(ids[i], 0, count - 1), 0)
                ),
            ],
            out_specs=pl.BlockSpec((BLOCK, width), lambda i, ids: (i, 0)),
        ),
        out_shape=jax.ShapeDtypeStruct((wanted * BLOCK, width), jnp.float32),
    )(ids, held)


def local(rows, cols, *arguments):
    inverses = arguments[0:4]
    couplings = arguments[4:8]
    inverse_root = arguments[8]
    sources = arguments[9:13]
    loads_root = arguments[13]
    target_blocks = arguments[14]
    links = Links(rows, cols)
    columns = loads_root.shape[1]
    parts = PARTS if columns % (PARTS * 128) == 0 else 1
    width = columns // parts
    children, count = target_blocks.shape
    per_row = couplings[0].shape[0] // BLOCK
    owned = loads_root.shape[0] // BLOCK
    held = inverse_root.shape[0] // BLOCK

    owned_ids = lax.axis_index("row") * owned + jnp.arange(owned, dtype=jnp.int32)
    same = target_blocks[:, :, None] == owned_ids[None, None, :]
    numbers = jnp.arange(count, dtype=jnp.int32)[None, :, None]
    slots = jnp.min(jnp.where(same, numbers, count), axis=1)
    mine = lax.dynamic_slice_in_dim(target_blocks, lax.axis_index("row") * per_row, per_row, 1)
    wanted = (mine - lax.axis_index("col") * held).reshape(-1)

    answers = []
    for part in range(parts):
        span = slice(part * width, (part + 1) * width)
        forward = [
            links.row_total(product(weight, source[:, span]))
            for weight, source in zip(inverses, sources)
        ]
        partial_value = jnp.concatenate(
            [product(weight, solved) for weight, solved in zip(couplings, forward)]
        )
        summed = links.col_scatter(partial_value)
        spread = links.core.gather(links.x.gather(links.col_gather(summed), 0), 1)
        blocks = spread.reshape(rows, children, per_row, BLOCK, width)
        blocks = blocks.transpose(1, 0, 2, 3, 4).reshape(children, count, BLOCK, width)
        shifted = place(loads_root, blocks, slots, part, parts)
        solved_root = links.row_total(product(inverse_root, shifted))
        picked = links.col_gather(links.col_scatter(take(solved_root, wanted)))
        picked = picked.reshape(children, per_row * BLOCK, width)
        finals = []
        for child in range(4):
            correction = links.row_total(transposed(couplings[child], picked[child]))
            final = transposed(inverses[child], forward[child] - correction)
            finals.append(links.col_scatter(final))
        answers.append(finals + [solved_root])
    return tuple(jnp.concatenate(list(pieces), axis=1) for pieces in zip(*answers))


def solution(mesh):
    rows, cols = mesh.shape["row"], mesh.shape["col"]
    matrices = [P("col", "row")] * 4 + [P("row", "col")] * 4 + [P("col", "row")]
    vectors = [P("row", None)] * 5
    return jax.shard_map(
        lambda *arguments: local(rows, cols, *arguments),
        mesh=mesh,
        in_specs=tuple(matrices + vectors + [P()]),
        out_specs=(P(AXES, None),) * 4 + (P("col", None),),
        check_vma=False,
    )
```

```python
import functools

import jax
import jax.numpy as jnp
from jax import lax
from jax.experimental import pallas as pl
from jax.experimental.pallas import tpu as pltpu
from jax.sharding import PartitionSpec as P

BLOCK = 128
AXES = ("row", "col")
LIMIT = 56 * 2**20


def product(matrix, vector):
    return jnp.dot(
        matrix, vector, precision=lax.Precision.HIGH, preferred_element_type=jnp.float32
    )


def transposed(matrix, vector):
    return lax.dot_general(
        matrix,
        vector,
        (((0,), (0,)), ((), ())),
        precision=lax.Precision.HIGH,
        preferred_element_type=jnp.float32,
    )


def pick(array, index, axis):
    return lax.dynamic_index_in_dim(array, index, axis, keepdims=False)


class Group:
    def __init__(self, rows, cols, axis, stride, size):
        self.size = size
        self.place = lax.rem(lax.axis_index(axis) // stride, size)
        self.pairs = []
        for step in range(1, size):
            listed = []
            for r in range(rows):
                for c in range(cols):
                    old = r if axis == "row" else c
                    digit = old // stride % size
                    new = old + ((digit + step) % size - digit) * stride
                    there = (new, c) if axis == "row" else (r, new)
                    listed.append((r * cols + c, there[0] * cols + there[1]))
            self.pairs.append(listed)

    def scatter_sum(self, array, axis):
        total = pick(array, self.place, axis)
        for step in range(1, self.size):
            sent = pick(array, lax.rem(self.place + step, self.size), axis)
            total = total + lax.ppermute(sent, AXES, self.pairs[step - 1])
        return total

    def gather(self, array, axis):
        if self.size == 1:
            return jnp.expand_dims(array, axis)
        held = [array]
        for step in range(1, self.size):
            held.append(lax.ppermute(array, AXES, self.pairs[step - 1]))
        if self.size == 2:
            first = self.place == 0
            return jnp.stack(
                [jnp.where(first, held[0], held[1]), jnp.where(first, held[1], held[0])], axis
            )
        shape = array.shape[:axis] + (self.size,) + array.shape[axis:]
        out = jnp.zeros(shape, array.dtype)
        for step, value in enumerate(held):
            source = lax.rem(self.place + self.size - step, self.size)
            out = lax.dynamic_update_index_in_dim(out, value, source, axis)
        return out

    def total(self, array):
        if self.size == 2:
            return array + lax.ppermute(array, AXES, self.pairs[0])
        if self.size == 1:
            return array
        pieces = array.reshape((self.size, array.shape[0] // self.size) + array.shape[1:])
        return self.gather(self.scatter_sum(pieces, 0), 0).reshape(array.shape)


class Links:
    def __init__(self, rows, cols):
        cores = 2 if rows % 2 == 0 else 1
        near = 1
        while cols % (near * 2) == 0 and near * near * 8 <= cols * 2:
            near *= 2
        self.core = Group(rows, cols, "row", 1, cores)
        self.x = Group(rows, cols, "row", cores, rows // cores)
        self.y = Group(rows, cols, "col", 1, near)
        self.z = Group(rows, cols, "col", near, cols // near)

    def row_total(self, array):
        pieces = array.reshape((self.core.size, array.shape[0] // self.core.size, array.shape[1]))
        part = self.x.total(self.core.scatter_sum(pieces, 0))
        return self.core.gather(part, 0).reshape(array.shape)

    def col_scatter(self, array):
        size = array.shape[0] // (self.z.size * self.y.size)
        pieces = array.reshape(self.z.size, self.y.size, size, array.shape[1])
        return self.z.scatter_sum(self.y.scatter_sum(pieces, 1), 0)

    def col_gather(self, array):
        whole = self.y.gather(self.z.gather(array, 0), 1)
        return whole.reshape(-1, array.shape[-1])


def place_kernel(count, map_ref, loads_ref, blocks_ref, out_ref):
    here = pl.program_id(0)
    out_ref[...] = loads_ref[...]
    for child in range(map_ref.shape[0]):
        source = map_ref[child, here]

        @pl.when(source < count)
        def _():
            out_ref[...] -= blocks_ref[child, source]


def place(loads, blocks, slots, part, parts):
    children, count, size, width = blocks.shape
    owned = slots.shape[1]
    return pl.pallas_call(
        lambda *refs: place_kernel(count, *refs),
        grid_spec=pltpu.PrefetchScalarGridSpec(
            num_scalar_prefetch=1,
            grid=(owned,),
            in_specs=[
                pl.BlockSpec((size, width), lambda i, slots: (i, part)),
                pl.BlockSpec((children, count, size, width), lambda i, slots: (0, 0, 0, 0)),
            ],
            out_specs=pl.BlockSpec((size, width), lambda i, slots: (i, 0)),
        ),
        out_shape=jax.ShapeDtypeStruct((owned * size, width), jnp.float32),
        compiler_params=pltpu.CompilerParams(vmem_limit_bytes=40 * 2**20),
    )(slots, loads, blocks)


def take_kernel(count, ids_ref, held_ref, out_ref):
    source = ids_ref[pl.program_id(0)]
    inside = jnp.logical_and(source >= 0, source < count)

    @pl.when(inside)
    def _():
        out_ref[...] = held_ref[...]

    @pl.when(jnp.logical_not(inside))
    def _():
        out_ref[...] = jnp.zeros_like(out_ref)


def take(held, ids):
    rows, width = held.shape
    count = rows // BLOCK
    wanted = ids.shape[0]
    return pl.pallas_call(
        lambda *refs: take_kernel(count, *refs),
        grid_spec=pltpu.PrefetchScalarGridSpec(
            num_scalar_prefetch=1,
            grid=(wanted,),
            in_specs=[
                pl.BlockSpec(
                    (BLOCK, width), lambda i, ids: (jnp.clip(ids[i], 0, count - 1), 0)
                ),
            ],
            out_specs=pl.BlockSpec((BLOCK, width), lambda i, ids: (i, 0)),
        ),
        out_shape=jax.ShapeDtypeStruct((wanted * BLOCK, width), jnp.float32),
    )(ids, held)


def general(rows, cols, *arguments):
    inverses = arguments[0:4]
    couplings = arguments[4:8]
    inverse_root = arguments[8]
    sources = arguments[9:13]
    loads_root = arguments[13]
    target_blocks = arguments[14]
    links = Links(rows, cols)
    columns = loads_root.shape[1]
    parts, width = 1, columns
    children, count = target_blocks.shape
    per_row = couplings[0].shape[0] // BLOCK
    owned = loads_root.shape[0] // BLOCK
    held = inverse_root.shape[0] // BLOCK

    owned_ids = lax.axis_index("row") * owned + jnp.arange(owned, dtype=jnp.int32)
    same = target_blocks[:, :, None] == owned_ids[None, None, :]
    numbers = jnp.arange(count, dtype=jnp.int32)[None, :, None]
    slots = jnp.min(jnp.where(same, numbers, count), axis=1)
    mine = lax.dynamic_slice_in_dim(target_blocks, lax.axis_index("row") * per_row, per_row, 1)
    wanted = (mine - lax.axis_index("col") * held).reshape(-1)

    answers = []
    for part in range(parts):
        span = slice(part * width, (part + 1) * width)
        forward = [
            links.row_total(product(weight, source[:, span]))
            for weight, source in zip(inverses, sources)
        ]
        partial_value = jnp.concatenate(
            [product(weight, solved) for weight, solved in zip(couplings, forward)]
        )
        summed = links.col_scatter(partial_value)
        spread = links.core.gather(links.x.gather(links.col_gather(summed), 0), 1)
        blocks = spread.reshape(rows, children, per_row, BLOCK, width)
        blocks = blocks.transpose(1, 0, 2, 3, 4).reshape(children, count, BLOCK, width)
        shifted = place(loads_root, blocks, slots, part, parts)
        solved_root = links.row_total(product(inverse_root, shifted))
        picked = links.col_gather(links.col_scatter(take(solved_root, wanted)))
        picked = picked.reshape(children, per_row * BLOCK, width)
        finals = []
        for child in range(4):
            correction = links.row_total(transposed(couplings[child], picked[child]))
            final = transposed(inverses[child], forward[child] - correction)
            finals.append(links.col_scatter(final))
        answers.append(finals + [solved_root])
    return tuple(jnp.concatenate(list(pieces), axis=1) for pieces in zip(*answers))


def split(value):
    high = value.astype(jnp.bfloat16)
    return high, (value - high.astype(jnp.float32)).astype(jnp.bfloat16)


def dot(first, second, flip=False):
    dims = (((0 if flip else 1,), (0,)), ((), ()))

    def one(a, b):
        return lax.dot_general(a, b, dims, preferred_element_type=jnp.float32)

    return one(first[0], second[0]) + (one(first[0], second[1]) + one(first[1], second[0]))


def call(kernel, me, inputs, outputs, scratch, macs):
    size = sum(a.size * 4 for a in inputs) + sum(4 * a.size for a in outputs)
    whole = pl.BlockSpec(memory_space=pltpu.VMEM)
    return pl.pallas_call(
        kernel,
        in_specs=[pl.BlockSpec(memory_space=pltpu.SMEM)] + [whole] * len(inputs),
        out_specs=[whole] * len(outputs),
        out_shape=outputs,
        scratch_shapes=scratch,
        cost_estimate=pl.CostEstimate(flops=6 * macs, bytes_accessed=size, transcendentals=0),
        compiler_params=pltpu.CompilerParams(vmem_limit_bytes=LIMIT),
    )(me, *inputs)


def shape(*extent):
    return jax.ShapeDtypeStruct(extent, jnp.float32)


def forward_kernel(me, first, second, first_loads, second_loads, own, other):
    width = own.shape[1]
    start = 0
    for weight, loads in ((first, first_loads), (second, second_loads)):
        rows = weight.shape[0]
        held = split(weight[...])
        for out, half in ((own, me[0]), (other, 1 - me[0])):
            part = loads[:, pl.ds(pl.multiple_of(half * width, width), width)]
            out[start : start + rows] = dot(held, split(part))
        start += rows


def couple_kernel(me, first, second, own, other, keep, send):
    y, z = me[1], me[2]
    count = keep.shape[0]
    start = 0
    for child, weight in enumerate((first, second)):
        rows = weight.shape[1]
        blocks = weight.shape[0] // BLOCK
        held = split(weight[...])
        mine, theirs = own[start : start + rows], other[start : start + rows]
        start += rows
        for out, half in ((send, 1 - y), (keep, y)):
            value = dot(held, split(jnp.where(half == 0, mine, theirs)))
            for block in range(blocks):
                place = lax.rem(child * blocks + block + count - z, count)
                out[place] = value[block * BLOCK : (block + 1) * BLOCK]


def base_kernel(me, weight, loads, own, other, high, low):
    width = own.shape[1]

    @pl.when(pl.program_id(0) == 0)
    def _():
        high[...], low[...] = split(loads[...])

    held = split(weight[...])
    for out, half in ((own, me[0]), (other, 1 - me[0])):
        span = pl.ds(pl.multiple_of(half * width, width), width)
        out[...] = dot(held, (high[:, span], low[:, span]))


def base(me, weight, loads):
    rows, depth = weight.shape
    columns = loads.shape[1]
    tile = rows // 8
    return pl.pallas_call(
        base_kernel,
        grid_spec=pltpu.PrefetchScalarGridSpec(
            num_scalar_prefetch=1,
            grid=(rows // tile,),
            in_specs=[
                pl.BlockSpec((tile, depth), lambda i, me: (i, 0)),
                pl.BlockSpec(memory_space=pltpu.VMEM),
            ],
            out_specs=[pl.BlockSpec((tile, columns // 2), lambda i, me: (i, 0))] * 2,
            scratch_shapes=[pltpu.VMEM((depth, columns), jnp.bfloat16)] * 2,
        ),
        out_shape=[shape(rows, columns // 2)] * 2,
        cost_estimate=pl.CostEstimate(
            flops=6 * rows * depth * columns,
            bytes_accessed=4 * (rows * depth + depth * columns + rows * columns),
            transcendentals=0,
        ),
        compiler_params=pltpu.CompilerParams(vmem_limit_bytes=LIMIT),
    )(me, weight, loads)


def root_kernel(list_ref, left, right, base_own, base_other, *refs):
    sources, outs, (moved,) = refs[:-5], refs[-5:-1], refs[-1:]
    step = pl.program_id(0)
    width = base_own.shape[1]
    rows = outs[0].shape[0]

    @pl.when(step == 0)
    def _():
        for piece in range(2):
            span = slice(piece * rows, (piece + 1) * rows)
            outs[piece][...] = base_own[span]
            outs[2 + piece][...] = base_other[span]

    @pl.when(2 * step < list_ref[4, 0])
    def _():
        for entry in range(2):
            span = slice(entry * BLOCK, (entry + 1) * BLOCK)
            which = list_ref[1, 2 * step + entry]

            @pl.when(which < 0)
            def _():
                moved[span] = jnp.zeros((BLOCK, 2 * width), jnp.float32)

            for number, source in enumerate(sources):

                @pl.when(which == number)
                def _():
                    moved[span, :width] = source[list_ref[2, 2 * step + entry]]
                    moved[span, width:] = source[list_ref[3, 2 * step + entry]]

        held = split(moved[...])
        tile = rows // 4
        for piece in range(2):
            for start in range(0, rows, tile):
                span = slice(piece * rows + start, piece * rows + start + tile)
                weight = split(jnp.concatenate([left[span], right[span]], axis=1))
                value = dot(weight, held)
                outs[piece][start : start + tile] -= value[:, :width]
                outs[2 + piece][start : start + tile] -= value[:, width:]


def root(listed, weight, bases, sources):
    rows = weight.shape[0]
    width = bases[0].shape[1]
    whole = pl.BlockSpec(memory_space=pltpu.VMEM)
    return pl.pallas_call(
        root_kernel,
        grid_spec=pltpu.PrefetchScalarGridSpec(
            num_scalar_prefetch=1,
            grid=(listed.shape[1] // 2,),
            in_specs=[
                pl.BlockSpec((rows, BLOCK), lambda i, listed: (0, listed[0, 2 * i])),
                pl.BlockSpec((rows, BLOCK), lambda i, listed: (0, listed[0, 2 * i + 1])),
            ]
            + [whole] * (2 + len(sources)),
            out_specs=[whole] * 4,
            scratch_shapes=[pltpu.VMEM((2 * BLOCK, 2 * width), jnp.float32)],
        ),
        out_shape=[shape(rows // 2, width)] * 4,
        cost_estimate=pl.CostEstimate(
            flops=6 * rows * 1024 * 2 * width,
            bytes_accessed=4 * (rows * 1024 + rows * width * 8),
            transcendentals=0,
        ),
        compiler_params=pltpu.CompilerParams(vmem_limit_bytes=LIMIT),
    )(listed, weight, weight, *bases, *sources)


def pick_kernel(me, first, second, keep, send):
    y, z = me[1], me[2]
    count = first.shape[0] // BLOCK
    children = keep.shape[0]
    for out, block in ((send, 1 - y), (keep, y)):
        for child in range(children):
            place = lax.rem(child + children - z, children)
            source = me[3 + 2 * child + block]
            inside = jnp.logical_and(source >= 0, source < 2 * count)

            @pl.when(jnp.logical_and(inside, source < count))
            def _():
                out[place] = first[pl.ds(pl.multiple_of(source * BLOCK, BLOCK), BLOCK)]

            @pl.when(jnp.logical_and(inside, source >= count))
            def _():
                start = pl.multiple_of((source - count) * BLOCK, BLOCK)
                out[place] = second[pl.ds(start, BLOCK)]

            @pl.when(jnp.logical_not(inside))
            def _():
                out[place] = jnp.zeros((BLOCK, first.shape[1]), jnp.float32)


def correct_kernel(pair, me, first, second, own_near, own_far, other_near, other_far, own, other, rows_ref):
    y, z = me[1], me[2]
    children = own_near.shape[0]
    near = pl.ds(pl.multiple_of(y * BLOCK, BLOCK), BLOCK)
    far = pl.ds(pl.multiple_of((1 - y) * BLOCK, BLOCK), BLOCK)
    start = 0
    for child, weight in zip(pair, (first, second)):
        rows = weight.shape[1]
        held = split(weight[...])
        place = lax.rem(z + children - child, children)
        for out, here, there in ((other, other_near, other_far), (own, own_near, own_far)):
            rows_ref[near] = here[place]
            rows_ref[far] = there[place]
            out[start : start + rows] = dot(held, split(rows_ref[...]), True)
        start += rows


def final_kernel(me, first, second, own, other, keep, send, whole):
    y, z = me[1], me[2]
    count = keep.shape[0]
    width = own.shape[1]
    start, place = 0, 0
    for weight in (first, second):
        rows, total = weight.shape
        size = total // (2 * count)
        held = split(weight[...])
        for half, vector in ((me[0], own), (1 - me[0], other)):
            columns = pl.ds(pl.multiple_of(half * width, width), width)
            whole[:total] = dot(held, split(vector[start : start + rows]), True)
            for out, side in ((send, 1 - y), (keep, y)):
                for owner in range(count):
                    taken = pl.ds(pl.multiple_of((2 * owner + side) * size, 8), size)
                    there = lax.rem(owner + count - z, count)
                    out[there, place : place + size, columns] = whole[taken]
        start += rows
        place += size


def fast(rows, cols, *arguments):
    inverses = arguments[0:4]
    couplings = arguments[4:8]
    inverse_root = arguments[8]
    sources = arguments[9:13]
    loads_root = arguments[13]
    target_blocks = arguments[14]
    links = Links(rows, cols)
    core, x, y, z = links.core, links.x, links.y, links.z
    width = loads_root.shape[1] // 2
    children, count = target_blocks.shape
    per_row = count // rows
    owned = loads_root.shape[0] // BLOCK
    held = inverse_root.shape[0] // BLOCK
    row = lax.axis_index("row")
    pairs = ((0, 3), (1, 2))

    def send(array, group, step=1):
        return lax.ppermute(array, AXES, group.pairs[step - 1])

    mine = lax.dynamic_slice_in_dim(target_blocks, row * per_row, per_row, 1)
    wanted = (mine - lax.axis_index("col") * held).reshape(-1)
    me = jnp.concatenate([jnp.stack([core.place, y.place, z.place]).astype(jnp.int32), wanted])

    child = jnp.arange(children, dtype=jnp.int32)[:, None] + jnp.zeros((1, count), jnp.int32)
    block = jnp.arange(count, dtype=jnp.int32)[None, :] + jnp.zeros((children, 1), jnp.int32)
    group = jnp.where((child == 0) | (child == 3), 0, 1)
    inner = jnp.where(child >= 2, 1, 0)
    from_row = block // per_row
    owner = inner * per_row + block % per_row
    away_x = jnp.where(from_row // 2 == x.place, 0, 1)
    away_core = jnp.where(from_row % 2 == core.place, 0, 1)
    array = group * 4 + away_core * 2 + away_x
    place = (z.place + z.size - owner) % z.size
    first = (away_core + y.place) % 2 * z.size + place
    second = (away_core + y.place + 1) % 2 * z.size + place
    local_block = target_blocks - row * owned
    inside = ((local_block >= 0) & (local_block < owned)).reshape(-1)
    rank = jnp.cumsum(inside.astype(jnp.int32)) - 1
    chosen = inside[None, :] & (rank[None, :] == jnp.arange(inside.shape[0])[:, None])
    table = jnp.stack([local_block, array + 1, first, second]).reshape(4, -1)
    listed = jnp.sum(jnp.where(chosen[None], table[:, None, :], 0), axis=2)
    listed = listed - jnp.array([[0], [1], [0], [0]], jnp.int32)
    found = jnp.sum(inside.astype(jnp.int32))
    entries = jnp.arange(inside.shape[0], dtype=jnp.int32)
    last = jnp.sum(jnp.where(entries == found - 1, listed[0], 0))
    listed = listed.at[0].set(jnp.where(entries < found, listed[0], last))
    listed = jnp.concatenate([listed, jnp.full((1, entries.size), found, jnp.int32)])

    forward, spread = [], []
    started = []
    for a, b in pairs:
        n = inverses[a].shape[0] + inverses[b].shape[0]
        macs = inverses[a].size + inverses[b].size
        started.append(
            call(
                forward_kernel,
                me,
                [inverses[a], inverses[b], sources[a], sources[b]],
                [shape(n, width)] * 2,
                [],
                macs * 2 * width,
            )
        )
    bases = base(me, inverse_root, loads_root)
    for (a, b), (own, other) in zip(pairs, started):
        own = own + send(other, core)
        own = own + send(own, x)
        other = send(own, core)
        forward.append((own, other))
        piece = shape(z.size, BLOCK, width)
        macs = couplings[a].size + couplings[b].size
        keep, sent = call(
            couple_kernel, me, [couplings[a], couplings[b], own, other], [piece] * 2, [], macs * 2 * width
        )
        part = keep + send(sent, y)
        total = part[0]
        for step in range(1, z.size):
            total = total + send(part[step], z, step)
        near = jnp.stack([total] + [send(total, z, step) for step in range(1, z.size)])
        near = jnp.concatenate([near, send(near, y)])
        far = send(near, x)
        spread += [near, far, send(near, core), send(far, core)]

    own0, own1, other0, other1 = root(listed, inverse_root, bases, spread)
    own0 = own0 + send(other0, core)
    own1 = own1 + send(other1, core)
    own0 = own0 + send(own0, x)
    own1 = own1 + send(own1, x)
    other0 = send(own0, core)
    other1 = send(own1, core)
    picked = []
    for pieces in ((own0, own1), (other0, other1)):
        piece = shape(children, BLOCK, width)
        keep, sent = call(pick_kernel, me, list(pieces), [piece] * 2, [], 0)
        part = keep + send(sent, y)
        total = part[0]
        for step in range(1, z.size):
            total = total + send(part[step], z, step)
        near = jnp.stack([total] + [send(total, z, step) for step in range(1, z.size)])
        picked += [near, send(near, y)]

    solved = [None] * 4
    for (a, b), (own, other) in zip(pairs, forward):
        macs = couplings[a].size + couplings[b].size
        fix_own, fix_other = call(
            functools.partial(correct_kernel, (a, b)),
            me,
            [couplings[a], couplings[b]] + picked,
            [shape(*own.shape)] * 2,
            [pltpu.VMEM((per_row * BLOCK, width), jnp.float32)],
            macs * 2 * width,
        )
        fix_own = fix_own + send(fix_other, core)
        own = own - fix_own - send(fix_own, x)
        other = send(own, core)
        sizes = [inverses[k].shape[1] // cols for k in (a, b)]
        piece = shape(z.size, sum(sizes), 2 * width)
        macs = inverses[a].size + inverses[b].size
        keep, sent = call(
            final_kernel,
            me,
            [inverses[a], inverses[b], own, other],
            [piece] * 2,
            [pltpu.VMEM((max(inverses[k].shape[1] for k in (a, b)), width), jnp.float32)],
            macs * 2 * width,
        )
        arrived = send(sent, y)
        total = keep[0] + arrived[0]
        for step in range(1, z.size):
            total = total + send(keep[step] + arrived[step], z, step)
        solved[a] = total[: sizes[0]]
        solved[b] = total[sizes[0] :]

    left = jnp.concatenate([own0, own1])
    right = jnp.concatenate([other0, other1])
    first = core.place == 0
    solved_root = jnp.concatenate(
        [jnp.where(first, left, right), jnp.where(first, right, left)], axis=1
    )
    return tuple(solved) + (solved_root,)


def local(rows, cols, *arguments):
    links = Links(rows, cols)
    children, count = arguments[14].shape
    columns = arguments[13].shape[1]
    sizes = [arguments[k].shape[1] for k in range(4)]
    fits = (
        links.core.size == 2
        and links.x.size == 2
        and links.y.size == 2
        and children == 4
        and links.z.size == 4
        and count == 2 * rows
        and arguments[4].shape[0] == 2 * BLOCK
        and columns % 256 == 0
        and arguments[8].shape[0] % (16 * BLOCK) == 0
        and all(size % (cols * 16) == 0 for size in sizes)
        and all(arguments[k].shape[0] % 16 == 0 for k in range(4))
    )
    return (fast if fits else general)(rows, cols, *arguments)


def solution(mesh):
    rows, cols = mesh.shape["row"], mesh.shape["col"]
    matrices = [P("col", "row")] * 4 + [P("row", "col")] * 4 + [P("col", "row")]
    vectors = [P("row", None)] * 5
    return jax.shard_map(
        lambda *arguments: local(rows, cols, *arguments),
        mesh=mesh,
        in_specs=tuple(matrices + vectors + [P()]),
        out_specs=(P(AXES, None),) * 4 + (P("col", None),),
        check_vma=False,
    )
```

```python
import functools

import jax
import jax.numpy as jnp
from jax import lax
from jax.experimental import pallas as pl
from jax.experimental.pallas import tpu as pltpu
from jax.sharding import PartitionSpec as P

BLOCK = 128
AXES = ("row", "col")
COST = pl.CostEstimate(flops=1, bytes_accessed=1, transcendentals=0)


def product(matrix, vector):
    return jnp.dot(
        matrix, vector, precision=lax.Precision.HIGH, preferred_element_type=jnp.float32
    )


def transposed(matrix, vector):
    return lax.dot_general(
        matrix,
        vector,
        (((0,), (0,)), ((), ())),
        precision=lax.Precision.HIGH,
        preferred_element_type=jnp.float32,
    )


def pick(array, index, axis):
    return lax.dynamic_index_in_dim(array, index, axis, keepdims=False)


class Group:
    def __init__(self, rows, cols, axis, stride, size):
        self.size = size
        self.place = lax.rem(lax.axis_index(axis) // stride, size)
        self.pairs = []
        for step in range(1, size):
            listed = []
            for r in range(rows):
                for c in range(cols):
                    old = r if axis == "row" else c
                    digit = old // stride % size
                    new = old + ((digit + step) % size - digit) * stride
                    there = (new, c) if axis == "row" else (r, new)
                    listed.append((r * cols + c, there[0] * cols + there[1]))
            self.pairs.append(listed)

    def scatter_sum(self, array, axis):
        total = pick(array, self.place, axis)
        for step in range(1, self.size):
            sent = pick(array, lax.rem(self.place + step, self.size), axis)
            total = total + lax.ppermute(sent, AXES, self.pairs[step - 1])
        return total

    def gather(self, array, axis):
        if self.size == 1:
            return jnp.expand_dims(array, axis)
        held = [array]
        for step in range(1, self.size):
            held.append(lax.ppermute(array, AXES, self.pairs[step - 1]))
        if self.size == 2:
            first = self.place == 0
            return jnp.stack(
                [jnp.where(first, held[0], held[1]), jnp.where(first, held[1], held[0])], axis
            )
        shape = array.shape[:axis] + (self.size,) + array.shape[axis:]
        out = jnp.zeros(shape, array.dtype)
        for step, value in enumerate(held):
            source = lax.rem(self.place + self.size - step, self.size)
            out = lax.dynamic_update_index_in_dim(out, value, source, axis)
        return out

    def total(self, array):
        if self.size == 2:
            return array + lax.ppermute(array, AXES, self.pairs[0])
        if self.size == 1:
            return array
        pieces = array.reshape((self.size, array.shape[0] // self.size) + array.shape[1:])
        return self.gather(self.scatter_sum(pieces, 0), 0).reshape(array.shape)


class Links:
    def __init__(self, rows, cols):
        cores = 2 if rows % 2 == 0 else 1
        near = 1
        while cols % (near * 2) == 0 and near * near * 8 <= cols * 2:
            near *= 2
        self.core = Group(rows, cols, "row", 1, cores)
        self.x = Group(rows, cols, "row", cores, rows // cores)
        self.y = Group(rows, cols, "col", 1, near)
        self.z = Group(rows, cols, "col", near, cols // near)

    def row_total(self, array):
        pieces = array.reshape((self.core.size, array.shape[0] // self.core.size, array.shape[1]))
        part = self.x.total(self.core.scatter_sum(pieces, 0))
        return self.core.gather(part, 0).reshape(array.shape)

    def col_scatter(self, array):
        size = array.shape[0] // (self.z.size * self.y.size)
        pieces = array.reshape(self.z.size, self.y.size, size, array.shape[1])
        return self.z.scatter_sum(self.y.scatter_sum(pieces, 1), 0)

    def col_gather(self, array):
        whole = self.y.gather(self.z.gather(array, 0), 1)
        return whole.reshape(-1, array.shape[-1])


def place_kernel(count, map_ref, loads_ref, blocks_ref, out_ref):
    here = pl.program_id(0)
    out_ref[...] = loads_ref[...]
    for child in range(map_ref.shape[0]):
        source = map_ref[child, here]

        @pl.when(source < count)
        def _():
            out_ref[...] -= blocks_ref[child, source]


def place(loads, blocks, slots, part, parts):
    children, count, size, width = blocks.shape
    owned = slots.shape[1]
    return pl.pallas_call(
        lambda *refs: place_kernel(count, *refs),
        grid_spec=pltpu.PrefetchScalarGridSpec(
            num_scalar_prefetch=1,
            grid=(owned,),
            in_specs=[
                pl.BlockSpec((size, width), lambda i, slots: (i, part)),
                pl.BlockSpec((children, count, size, width), lambda i, slots: (0, 0, 0, 0)),
            ],
            out_specs=pl.BlockSpec((size, width), lambda i, slots: (i, 0)),
        ),
        out_shape=jax.ShapeDtypeStruct((owned * size, width), jnp.float32),
        compiler_params=pltpu.CompilerParams(vmem_limit_bytes=40 * 2**20),
    )(slots, loads, blocks)


def take_kernel(count, ids_ref, held_ref, out_ref):
    source = ids_ref[pl.program_id(0)]
    inside = jnp.logical_and(source >= 0, source < count)

    @pl.when(inside)
    def _():
        out_ref[...] = held_ref[...]

    @pl.when(jnp.logical_not(inside))
    def _():
        out_ref[...] = jnp.zeros_like(out_ref)


def take(held, ids):
    rows, width = held.shape
    count = rows // BLOCK
    wanted = ids.shape[0]
    return pl.pallas_call(
        lambda *refs: take_kernel(count, *refs),
        grid_spec=pltpu.PrefetchScalarGridSpec(
            num_scalar_prefetch=1,
            grid=(wanted,),
            in_specs=[
                pl.BlockSpec(
                    (BLOCK, width), lambda i, ids: (jnp.clip(ids[i], 0, count - 1), 0)
                ),
            ],
            out_specs=pl.BlockSpec((BLOCK, width), lambda i, ids: (i, 0)),
        ),
        out_shape=jax.ShapeDtypeStruct((wanted * BLOCK, width), jnp.float32),
    )(ids, held)


def general(rows, cols, *arguments):
    inverses = arguments[0:4]
    couplings = arguments[4:8]
    inverse_root = arguments[8]
    sources = arguments[9:13]
    loads_root = arguments[13]
    target_blocks = arguments[14]
    links = Links(rows, cols)
    columns = loads_root.shape[1]
    parts, width = 1, columns
    children, count = target_blocks.shape
    per_row = couplings[0].shape[0] // BLOCK
    owned = loads_root.shape[0] // BLOCK
    held = inverse_root.shape[0] // BLOCK

    owned_ids = lax.axis_index("row") * owned + jnp.arange(owned, dtype=jnp.int32)
    same = target_blocks[:, :, None] == owned_ids[None, None, :]
    numbers = jnp.arange(count, dtype=jnp.int32)[None, :, None]
    slots = jnp.min(jnp.where(same, numbers, count), axis=1)
    mine = lax.dynamic_slice_in_dim(target_blocks, lax.axis_index("row") * per_row, per_row, 1)
    wanted = (mine - lax.axis_index("col") * held).reshape(-1)

    answers = []
    for part in range(parts):
        span = slice(part * width, (part + 1) * width)
        forward = [
            links.row_total(product(weight, source[:, span]))
            for weight, source in zip(inverses, sources)
        ]
        partial_value = jnp.concatenate(
            [product(weight, solved) for weight, solved in zip(couplings, forward)]
        )
        summed = links.col_scatter(partial_value)
        spread = links.core.gather(links.x.gather(links.col_gather(summed), 0), 1)
        blocks = spread.reshape(rows, children, per_row, BLOCK, width)
        blocks = blocks.transpose(1, 0, 2, 3, 4).reshape(children, count, BLOCK, width)
        shifted = place(loads_root, blocks, slots, part, parts)
        solved_root = links.row_total(product(inverse_root, shifted))
        picked = links.col_gather(links.col_scatter(take(solved_root, wanted)))
        picked = picked.reshape(children, per_row * BLOCK, width)
        finals = []
        for child in range(4):
            correction = links.row_total(transposed(couplings[child], picked[child]))
            final = transposed(inverses[child], forward[child] - correction)
            finals.append(links.col_scatter(final))
        answers.append(finals + [solved_root])
    return tuple(jnp.concatenate(list(pieces), axis=1) for pieces in zip(*answers))


def split(value):
    high = value.astype(jnp.bfloat16)
    return high, (value - high.astype(jnp.float32)).astype(jnp.bfloat16)


def dot(first, second, flip=False):
    dims = (((0 if flip else 1,), (0,)), ((), ()))

    def one(a, b):
        return lax.dot_general(a, b, dims, preferred_element_type=jnp.float32)

    return one(first[0], second[0]) + (one(first[0], second[1]) + one(first[1], second[0]))


class Sequence:
    def __init__(self, me):
        self.me = me
        self.last = me

    def __call__(self, kernel, inputs, outputs, scratch=(), limit=24):
        whole = pl.BlockSpec(memory_space=pltpu.VMEM)
        count = len(inputs)
        results = pl.pallas_call(
            lambda *refs: kernel(*refs[: count + 1], *refs[count + 2 :]),
            in_specs=[pl.BlockSpec(memory_space=pltpu.SMEM)]
            + [whole] * count
            + [pl.BlockSpec(memory_space=pl.ANY)],
            out_specs=[whole] * len(outputs),
            out_shape=list(outputs),
            scratch_shapes=list(scratch),
            cost_estimate=COST,
            compiler_params=pltpu.CompilerParams(vmem_limit_bytes=limit * 2**20),
        )(self.me, *inputs, self.last)
        self.last = results[0]
        return results

    def merge(self, inputs, signs=None):
        signs = signs or (1,) * len(inputs)

        def kernel(me, *refs):
            refs[-1][...] = total([ref[...] for ref in refs[:-1]], signs)

        return self(kernel, inputs, [shape(*inputs[0].shape)])[0]

    def merge_split(self, inputs):
        count = inputs[0].shape[0]

        def kernel(me, *refs):
            sources, outs = refs[: len(inputs)], refs[len(inputs) :]
            for place in range(count):
                outs[place][...] = total([ref[place] for ref in sources], (1,) * len(inputs))

        return self(kernel, inputs, [shape(*inputs[0].shape[1:])] * count)

    def stack(self, inputs):
        def kernel(me, *refs):
            for place, ref in enumerate(refs[:-1]):
                refs[-1][place] = ref[...]

        return self(kernel, inputs, [shape(len(inputs), *inputs[0].shape)])[0]

    def join(self, inputs):
        rows = [a.shape[0] for a in inputs]

        def kernel(me, *refs):
            start = 0
            for ref, count in zip(refs[:-1], rows):
                refs[-1][start : start + count] = ref[...]
                start += count

        return self(kernel, inputs, [shape(sum(rows), *inputs[0].shape[1:])])[0]


def total(values, signs):
    result = values[0]
    for value, sign in zip(values[1:], signs[1:]):
        result = result + value if sign > 0 else result - value
    return result


def shape(*extent):
    return jax.ShapeDtypeStruct(extent, jnp.float32)


def part_of(half, part, width):
    parts = 2
    return pl.ds(pl.multiple_of((half * parts + part) * width, width), width)


def forward_kernel(parts, me, *refs):
    count = (len(refs) - 2 * len(parts)) // 2
    outs = refs[2 * count :]
    width = outs[0].shape[1]
    start = 0
    for weight, loads in zip(refs[:count], refs[count : 2 * count]):
        rows = weight.shape[0]
        pieces = [
            loads[:, part_of(half, part, width)] for part in parts for half in (me[0], 1 - me[0])
        ]
        value = dot(split(weight[...]), split(jnp.concatenate(pieces, axis=1)))
        for place, out in enumerate(outs):
            out[start : start + rows] = value[:, place * width : (place + 1) * width]
        start += rows


def couple_kernel(me, *refs):
    y, z = me[1], me[2]
    keep, send = refs[-2:]
    count = keep.shape[0]
    for child in range(count):
        weight, (own, other, start) = refs[child], refs[count + child]
        rows = weight.shape[1]
        span = slice(start, start + rows)
        held = jnp.concatenate([own[span], other[span]], axis=1)
        value = dot(split(weight[...]), split(held))
        place = lax.rem(child + count - z, count)

        @pl.when(y == 0)
        def _():
            keep[place] = value[:BLOCK]
            send[place] = value[BLOCK:]

        @pl.when(y != 0)
        def _():
            keep[place] = value[BLOCK:]
            send[place] = value[:BLOCK]


def base_kernel(me, weight, mine, theirs, last, out, high, low):
    @pl.when(pl.program_id(0) == 0)
    def _():
        high[...], low[...] = split(jnp.concatenate([mine[...], theirs[...]], axis=1))

    out[...] = dot(split(weight[...]), (high[...], low[...]))


def base(sequence, part, piece, width, weight, loads):
    rows, depth = weight.shape[0] // 2, weight.shape[1]
    steps = 4
    tile = rows // steps
    parts = 2
    result = pl.pallas_call(
        base_kernel,
        grid_spec=pltpu.PrefetchScalarGridSpec(
            num_scalar_prefetch=1,
            grid=(steps,),
            in_specs=[
                pl.BlockSpec((tile, depth), lambda i, me: (piece * steps + i, 0)),
                pl.BlockSpec((depth, width), lambda i, me: (0, me[0] * parts + part)),
                pl.BlockSpec((depth, width), lambda i, me: (0, (1 - me[0]) * parts + part)),
                pl.BlockSpec(memory_space=pl.ANY),
            ],
            out_specs=pl.BlockSpec((tile, 2 * width), lambda i, me: (i, 0)),
            scratch_shapes=[pltpu.VMEM((depth, 2 * width), jnp.bfloat16)] * 2,
        ),
        out_shape=shape(rows, 2 * width),
        cost_estimate=COST,
        compiler_params=pltpu.CompilerParams(vmem_limit_bytes=40 * 2**20),
    )(sequence.me, weight, loads, loads, sequence.last)
    sequence.last = result
    return result


def root_kernel(list_ref, left, right, upper, lower, *refs):
    sources, (own, other, moved) = refs[:-4], refs[-3:]
    step = pl.program_id(0)
    width = own.shape[1]
    rows = own.shape[0]

    @pl.when(step == 0)
    def _():
        for start, ref in ((0, upper), (rows // 2, lower)):
            own[start : start + rows // 2] = ref[:, :width]
            other[start : start + rows // 2] = ref[:, width:]

    @pl.when(2 * step < list_ref[3, 0])
    def _():
        for entry in range(2):
            span = slice(entry * BLOCK, (entry + 1) * BLOCK)
            which = list_ref[1, 2 * step + entry]
            place = list_ref[2, 2 * step + entry]

            @pl.when(which < 0)
            def _():
                moved[span] = jnp.zeros((BLOCK, 2 * width), jnp.float32)

            for number, source in enumerate(sources):

                @pl.when(which == number)
                def _():
                    if number < 2:
                        moved[span] = source[place]
                    else:
                        moved[span, :width] = source[place, :, width:]
                        moved[span, width:] = source[place, :, :width]

        held = split(moved[...])
        tile = rows // 4
        for start in range(0, rows, tile):
            span = slice(start, start + tile)
            weight = split(jnp.concatenate([left[span], right[span]], axis=1))
            value = dot(weight, held)
            own[span] -= value[:, :width]
            other[span] -= value[:, width:]


def root(sequence, listed, weight, starts, sources):
    rows = weight.shape[0]
    width = starts[0].shape[1] // 2
    whole = pl.BlockSpec(memory_space=pltpu.VMEM)
    results = pl.pallas_call(
        root_kernel,
        grid_spec=pltpu.PrefetchScalarGridSpec(
            num_scalar_prefetch=1,
            grid=(listed.shape[1] // 2,),
            in_specs=[
                pl.BlockSpec((rows, BLOCK), lambda i, listed: (0, listed[0, 2 * i])),
                pl.BlockSpec((rows, BLOCK), lambda i, listed: (0, listed[0, 2 * i + 1])),
            ]
            + [whole] * (2 + len(sources))
            + [pl.BlockSpec(memory_space=pl.ANY)],
            out_specs=[whole] * 2,
            scratch_shapes=[pltpu.VMEM((2 * BLOCK, 2 * width), jnp.float32)],
        ),
        out_shape=[shape(rows, width)] * 2,
        cost_estimate=COST,
        compiler_params=pltpu.CompilerParams(vmem_limit_bytes=40 * 2**20),
    )(listed, weight, weight, *starts, *sources, sequence.last)
    sequence.last = results[0]
    return results


def pick_kernel(me, own, other, keep, send):
    y, z = me[1], me[2]
    count = own.shape[0] // BLOCK
    width = own.shape[1]
    children = keep.shape[0]
    for out, block in ((send, 1 - y), (keep, y)):
        for child in range(children):
            place = lax.rem(child + children - z, children)
            source = me[3 + 2 * child + block]
            inside = jnp.logical_and(source >= 0, source < count)

            @pl.when(inside)
            def _():
                span = pl.ds(pl.multiple_of(source * BLOCK, BLOCK), BLOCK)
                out[place, :, :width] = own[span]
                out[place, :, width:] = other[span]

            @pl.when(jnp.logical_not(inside))
            def _():
                out[place] = jnp.zeros((BLOCK, 2 * width), jnp.float32)


def correct_kernel(pair, me, first, second, near, far, own, other, rows_ref):
    y, z = me[1], me[2]
    width = own.shape[1]
    children = near.shape[0]
    start = 0
    for child, weight in zip(pair, (first, second)):
        rows = weight.shape[1]
        place = lax.rem(z + children - child, children)
        rows_ref[pl.ds(pl.multiple_of(y * BLOCK, BLOCK), BLOCK)] = near[place]
        rows_ref[pl.ds(pl.multiple_of((1 - y) * BLOCK, BLOCK), BLOCK)] = far[place]
        value = dot(split(weight[...]), split(rows_ref[...]), True)
        own[start : start + rows] = value[:, :width]
        other[start : start + rows] = value[:, width:]
        start += rows


def final_kernel(me, first, second, own, other, keep, send, whole):
    y, z = me[1], me[2]
    count = keep.shape[0]
    width = own.shape[1]
    start, place = 0, 0
    for weight in (first, second):
        rows, columns = weight.shape
        size = columns // (2 * count)
        span = slice(start, start + rows)
        held = jnp.concatenate([own[span], other[span]], axis=1)
        value = dot(split(weight[...]), split(held), True)
        whole[:columns, pl.ds(pl.multiple_of(me[0] * width, width), width)] = value[:, :width]
        whole[:columns, pl.ds(pl.multiple_of((1 - me[0]) * width, width), width)] = value[:, width:]
        for out, side in ((send, 1 - y), (keep, y)):
            for owner in range(count):
                taken = pl.ds(pl.multiple_of((2 * owner + side) * size, 8), size)
                out[jnp.bitwise_xor(owner, z), place : place + size] = whole[taken]
        start += rows
        place += size


def halve_kernel(me, keep, arrived, send, held):
    for place in range(keep.shape[0]):
        out = send if place % 2 else held
        out[place // 2] = keep[place] + arrived[place]


def finish_kernel(terms, me, *refs):
    parts = len(terms)
    held = iter(refs[:-2])
    first, second = refs[-2:]
    rows = first.shape[0]
    width = first.shape[1] // (2 * parts)
    for part in range(parts):
        value = total([next(held)[...] for _ in range(terms[part])], (1,) * terms[part])
        for half in range(2):
            there = slice((half * parts + part) * width, (half * parts + part + 1) * width)
            here = slice(half * width, (half + 1) * width)
            first[:, there] = value[:rows, here]
            second[:, there] = value[rows:, here]


def whole_kernel(me, *refs):
    out = refs[-1]
    width = refs[0].shape[1]
    for part in range(2):
        out[:, part_of(me[0], part, width)] = refs[2 * part][...]
        out[:, part_of(1 - me[0], part, width)] = refs[2 * part + 1][...]


def fast(rows, cols, *arguments):
    inverses = arguments[0:4]
    couplings = arguments[4:8]
    inverse_root = arguments[8]
    sources = arguments[9:13]
    loads_root = arguments[13]
    target_blocks = arguments[14]
    links = Links(rows, cols)
    core, x, y, z = links.core, links.x, links.y, links.z
    width = loads_root.shape[1] // 4
    children, count = target_blocks.shape
    per_row = count // rows
    owned = loads_root.shape[0] // BLOCK
    held = inverse_root.shape[0] // BLOCK
    row = lax.axis_index("row")
    pairs = ((0, 3), (1, 2))

    def send(array, group, step=1):
        return lax.ppermute(array, AXES, group.pairs[step - 1])

    def spread(array, group):
        return [send(array, group, step) for step in range(1, group.size)]

    def deal(arrays, group):
        return [send(arrays[step], group, step) for step in range(1, group.size)]

    mine = lax.dynamic_slice_in_dim(target_blocks, row * per_row, per_row, 1)
    wanted = (mine - lax.axis_index("col") * held).reshape(-1)
    me = jnp.concatenate([jnp.stack([core.place, y.place, z.place]).astype(jnp.int32), wanted])

    child = jnp.arange(children, dtype=jnp.int32)[:, None] + jnp.zeros((1, count), jnp.int32)
    block = jnp.arange(count, dtype=jnp.int32)[None, :] + jnp.zeros((children, 1), jnp.int32)
    from_row = block // per_row
    away_x = jnp.where(from_row // 2 == x.place, 0, 1)
    away_core = jnp.where(from_row % 2 == core.place, 0, 1)
    away_y = jnp.where(block % per_row == y.place, 0, 1)
    place = (z.place + z.size - child) % z.size
    local_block = target_blocks - row * owned
    inside = ((local_block >= 0) & (local_block < owned)).reshape(-1)
    rank = jnp.cumsum(inside.astype(jnp.int32)) - 1
    entries = jnp.arange(inside.shape[0], dtype=jnp.int32)
    chosen = inside[None, :] & (rank[None, :] == entries[:, None])
    tables = (
        (local_block, away_core * 2 + away_x + 1, away_y * z.size + place),
        (local_block, away_core * 2 + away_y + 1, place * x.size + away_x),
    )
    found = jnp.sum(inside.astype(jnp.int32))
    listed = []
    for table in tables:
        rows_of = jnp.stack(table).reshape(3, -1)
        held_rows = jnp.sum(jnp.where(chosen[None], rows_of[:, None, :], 0), axis=2)
        last = jnp.sum(jnp.where(entries == found - 1, held_rows[0], 0))
        listed.append(
            jnp.stack(
                [
                    jnp.where(entries < found, held_rows[0], last),
                    held_rows[1] - 1,
                    held_rows[2],
                    jnp.zeros_like(entries) + found,
                ]
            )
        )

    run = Sequence(me)
    parts = range(2)
    state = [dict() for _ in parts]

    def forward_start(pair, chosen):
        weights = [inverses[k] for k in pair]
        loads = [sources[k] for k in pair]
        n = sum(weight.shape[0] for weight in weights)
        outs = run(
            functools.partial(forward_kernel, chosen),
            weights + loads,
            [shape(n, width)] * (2 * len(chosen)),
            limit=56,
        )
        return [(own, send(other, core)) for own, other in zip(outs[::2], outs[1::2])]

    def forward_cross(own, arrived):
        own = run.merge([own, arrived])
        return own, send(own, x)

    def forward_end(own, arrived):
        own = run.merge([own, arrived])
        return own, send(own, core)

    def couple(part, arrays):
        flat = [a for own, other, _ in arrays for a in (own, other)]
        firsts = [start for _, _, start in arrays]

        def kernel(me, *refs):
            held = refs[children : 3 * children]
            triples = [(held[2 * k], held[2 * k + 1], firsts[k]) for k in range(children)]
            couple_kernel(me, *refs[:children], *triples, *refs[3 * children :])

        piece = shape(z.size, BLOCK, 2 * width)
        keep, sent = run(kernel, list(couplings) + flat, [piece] * 2, limit=40)
        state[part]["keep"], state[part]["arrived"] = keep, send(sent, y)

    def sum_y(part):
        split_up = run.merge_split([state[part]["keep"], state[part]["arrived"]])
        state[part]["terms"] = [split_up[0]] + deal(split_up, z)

    def sum_z(part):
        value = run.merge(state[part]["terms"])
        state[part]["pieces"] = [value] + spread(value, z)

    def gather_z(part):
        near = run.stack(state[part]["pieces"])
        state[part]["near"], state[part]["far"] = near, send(near, y)

    def gather_y(part):
        near = run.join([state[part]["near"], state[part]["far"]])
        far = send(near, x)
        state[part]["blocks"] = [near, far, send(near, core), send(far, core)]

    def gather_x(part):
        value = run.merge(state[part]["terms"])
        state[part]["pieces"] = [value, send(value, x)]

    def spread_z(part):
        both = run.stack(state[part]["pieces"])
        state[part]["pieces"] = [both] + spread(both, z)

    def join_z(part):
        near = run.join(state[part]["pieces"])
        far = send(near, y)
        state[part]["blocks"] = [near, far, send(near, core), send(far, core)]

    def solve_root(part):
        own, other = root(run, listed[part], inverse_root, state[part]["base"], state[part]["blocks"])
        state[part]["root"] = own, send(other, core)

    def cross_root(part):
        own = run.merge(list(state[part]["root"]))
        state[part]["root"] = own, send(own, x)

    def end_root(part):
        own = run.merge(list(state[part]["root"]))
        state[part]["root"] = own, send(own, core)

    def pick_root(part):
        piece = shape(children, BLOCK, 2 * width)
        keep, sent = run(pick_kernel, list(state[part]["root"]), [piece] * 2)
        state[part]["keep"], state[part]["arrived"] = keep, send(sent, y)

    def correct(part, group):
        pair = pairs[group]
        weights = [couplings[k] for k in pair]
        own, other = run(
            functools.partial(correct_kernel, pair),
            weights + [state[part]["near"], state[part]["far"]],
            [shape(sum(weight.shape[1] for weight in weights), width)] * 2,
            [pltpu.VMEM((per_row * BLOCK, 2 * width), jnp.float32)],
        )
        state[part][group] = own, send(other, core)

    def correct_cross(part, group):
        own = run.merge(list(state[part][group]))
        state[part][group] = own, send(own, x)

    def reduce(part, group):
        first = forward[part][group][0]
        own = run.merge([first] + list(state[part][group]), (1, -1, -1))
        state[part][group] = own, send(own, core)

    def final(part, group):
        weights = [inverses[k] for k in pairs[group]]
        size = sum(weight.shape[1] for weight in weights) // cols
        keep, sent = run(
            final_kernel,
            weights + list(state[part][group]),
            [shape(z.size, size, 2 * width)] * 2,
            [pltpu.VMEM((max(weight.shape[1] for weight in weights), 2 * width), jnp.float32)],
            limit=40,
        )
        state[part][group] = keep, send(sent, y)

    def exchange(array, mask):
        flip = mask * y.size
        listed = [(r * cols + c, r * cols + (c ^ flip)) for r in range(rows) for c in range(cols)]
        return lax.ppermute(array, AXES, listed)

    def final_y(part, group):
        keep, arrived = state[part][group]
        half = shape(z.size // 2, *keep.shape[1:])
        sent, held = run(halve_kernel, [keep, arrived], [half] * 2)
        state[part][group] = held, exchange(sent, 1)

    def final_z(part, group):
        held, away = run.merge_split(list(state[part][group]))
        state[part][group] = [held, exchange(away, 2)]

    def finish(group):
        sizes = [inverses[k].shape[1] // cols for k in pairs[group]]
        outs = [shape(size, 4 * width) for size in sizes]
        terms = [len(state[part][group]) for part in parts]
        inputs = [a for part in parts for a in state[part][group]]
        return run(functools.partial(finish_kernel, terms), inputs, outs)

    def final_last(part, group):
        state[part][group] = [run.merge(state[part][group])]

    def by_child(part):
        arrays = [None] * children
        for (a, b), (own, other) in zip(pairs, forward[part]):
            arrays[a] = own, other, 0
            arrays[b] = own, other, couplings[a].shape[1]
        return arrays

    def start_root(part, piece):
        held = base(run, part, piece, width, inverse_root, loads_root)
        state[part].setdefault("base", []).append(held)

    def forward_begin(chosen):
        begun = [forward_start(pair, chosen) for pair in pairs]
        return [[forward_cross(*pieces[k]) for pieces in begun] for k in range(len(chosen))]

    crossed = forward_begin((0, 1))
    start_root(0, 0)
    start_root(0, 1)
    forward = [None, None]
    forward[0] = [forward_end(*piece) for piece in crossed[0]]
    couple(0, by_child(0))
    start_root(1, 0)
    sum_y(0)
    start_root(1, 1)
    sum_z(0)
    forward[1] = [forward_end(*piece) for piece in crossed[1]]
    couple(1, by_child(1))
    gather_z(0)
    sum_y(1)
    gather_y(0)
    gather_x(1)
    spread_z(1)
    solve_root(0)
    join_z(1)
    cross_root(0)
    end_root(0)
    solve_root(1)
    pick_root(0)
    cross_root(1)
    sum_y(0)
    end_root(1)
    sum_z(0)
    pick_root(1)
    gather_z(0)
    sum_y(1)
    (solved_root,) = run(
        whole_kernel,
        [a for part in parts for a in state[part]["root"]],
        [shape(inverse_root.shape[0], 4 * width)],
    )
    correct(0, 0)
    correct(0, 1)
    correct_cross(0, 0)
    correct_cross(0, 1)
    sum_z(1)
    reduce(0, 0)
    gather_z(1)
    final(0, 0)
    reduce(0, 1)
    correct(1, 0)
    correct(1, 1)
    final(0, 1)
    correct_cross(1, 0)
    correct_cross(1, 1)
    final_y(0, 0)
    reduce(1, 0)
    final_z(0, 0)
    final(1, 0)
    reduce(1, 1)
    final_y(0, 1)
    final(1, 1)
    final_last(0, 0)
    final_z(0, 1)
    final_y(1, 0)
    final_last(0, 1)
    final_z(1, 0)
    final_y(1, 1)
    final_last(1, 0)
    final_z(1, 1)
    solved = [None] * 4
    for group, (a, b) in enumerate(pairs):
        solved[a], solved[b] = finish(group)
    return tuple(solved) + (solved_root,)


def local(rows, cols, *arguments):
    links = Links(rows, cols)
    children, count = arguments[14].shape
    columns = arguments[13].shape[1]
    sizes = [arguments[k].shape[1] for k in range(4)]
    fits = (
        links.core.size == 2
        and links.x.size == 2
        and links.y.size == 2
        and children == 4
        and links.z.size == 4
        and count == 2 * rows
        and arguments[4].shape[0] == 2 * BLOCK
        and columns % 512 == 0
        and arguments[8].shape[0] % (16 * BLOCK) == 0
        and all(size % (cols * 16) == 0 for size in sizes)
        and all(arguments[k].shape[0] % 16 == 0 for k in range(4))
    )
    return (fast if fits else general)(rows, cols, *arguments)


def solution(mesh):
    rows, cols = mesh.shape["row"], mesh.shape["col"]
    matrices = [P("col", "row")] * 4 + [P("row", "col")] * 4 + [P("col", "row")]
    vectors = [P("row", None)] * 5
    return jax.shard_map(
        lambda *arguments: local(rows, cols, *arguments),
        mesh=mesh,
        in_specs=tuple(matrices + vectors + [P()]),
        out_specs=(P(AXES, None),) * 4 + (P("col", None),),
        check_vma=False,
    )
```

```python
import functools

import jax
import jax.numpy as jnp
from jax import lax
from jax.experimental import pallas as pl
from jax.experimental.pallas import tpu as pltpu
from jax.sharding import PartitionSpec as P

BLOCK = 128
AXES = ("row", "col")
COST = pl.CostEstimate(flops=1, bytes_accessed=1, transcendentals=0)

ORDER = (
    ("begin", 0),
    ("begin", 1),
    ("cross", 0, 0),
    ("cross", 0, 1),
    ("cross", 1, 0),
    ("cross", 1, 1),
    ("base", 0, 0),
    ("base", 0, 1),
    ("end", 0, 0),
    ("end", 0, 1),
    ("couple", 0),
    ("base", 1, 0),
    ("sum_y", 0),
    ("base", 1, 1),
    ("sum_z", 0),
    ("end", 1, 0),
    ("end", 1, 1),
    ("couple", 1),
    ("sum_y", 1),
    ("gather_z", 0),
    ("gather_y", 0),
    ("sum_z", 1),
    ("gather_z", 1),
    ("hold_far", 0),
    ("root", 0),
    ("cross_root", 0),
    ("gather_y", 1),
    ("end_root", 0),
    ("pick", 0),
    ("pick_y", 0),
    ("hold_far", 1),
    ("root", 1),
    ("pick_z", 0),
    ("cross_root", 1),
    ("pick_g", 0),
    ("end_root", 1),
    ("pick", 1),
    ("correct", 0, 0),
    ("correct", 0, 1),
    ("correct_x", 0, 0),
    ("correct_x", 0, 1),
    ("pick_y", 1),
    ("pick_z", 1),
    ("reduce", 0, 0),
    ("final", 0, 0),
    ("whole",),
    ("pick_g", 1),
    ("final_y", 0, 0),
    ("reduce", 0, 1),
    ("final", 0, 1),
    ("correct", 1, 0),
    ("correct", 1, 1),
    ("correct_x", 1, 0),
    ("correct_x", 1, 1),
    ("final_z", 0, 0),
    ("reduce", 1, 0),
    ("final", 1, 0),
    ("final_y", 0, 1),
    ("reduce", 1, 1),
    ("final", 1, 1),
    ("final_last", 0, 0),
    ("final_z", 0, 1),
    ("final_y", 1, 0),
    ("final_last", 0, 1),
    ("final_y", 1, 2),
    ("final_y", 1, 3),
    ("final_z", 1, 0),
    ("final_z", 1, 2),
    ("final_last", 1, 0),
    ("final_z", 1, 3),
    ("finish", 0),
    ("finish", 1),
)


def product(matrix, vector):
    return jnp.dot(
        matrix, vector, precision=lax.Precision.HIGH, preferred_element_type=jnp.float32
    )


def transposed(matrix, vector):
    return lax.dot_general(
        matrix,
        vector,
        (((0,), (0,)), ((), ())),
        precision=lax.Precision.HIGH,
        preferred_element_type=jnp.float32,
    )


def pick(array, index, axis):
    return lax.dynamic_index_in_dim(array, index, axis, keepdims=False)


class Group:
    def __init__(self, rows, cols, axis, stride, size):
        self.size = size
        self.place = lax.rem(lax.axis_index(axis) // stride, size)
        self.pairs = []
        for step in range(1, size):
            listed = []
            for r in range(rows):
                for c in range(cols):
                    old = r if axis == "row" else c
                    digit = old // stride % size
                    new = old + ((digit + step) % size - digit) * stride
                    there = (new, c) if axis == "row" else (r, new)
                    listed.append((r * cols + c, there[0] * cols + there[1]))
            self.pairs.append(listed)

    def scatter_sum(self, array, axis):
        total = pick(array, self.place, axis)
        for step in range(1, self.size):
            sent = pick(array, lax.rem(self.place + step, self.size), axis)
            total = total + lax.ppermute(sent, AXES, self.pairs[step - 1])
        return total

    def gather(self, array, axis):
        if self.size == 1:
            return jnp.expand_dims(array, axis)
        held = [array]
        for step in range(1, self.size):
            held.append(lax.ppermute(array, AXES, self.pairs[step - 1]))
        if self.size == 2:
            first = self.place == 0
            return jnp.stack(
                [jnp.where(first, held[0], held[1]), jnp.where(first, held[1], held[0])], axis
            )
        shape = array.shape[:axis] + (self.size,) + array.shape[axis:]
        out = jnp.zeros(shape, array.dtype)
        for step, value in enumerate(held):
            source = lax.rem(self.place + self.size - step, self.size)
            out = lax.dynamic_update_index_in_dim(out, value, source, axis)
        return out

    def total(self, array):
        if self.size == 2:
            return array + lax.ppermute(array, AXES, self.pairs[0])
        if self.size == 1:
            return array
        pieces = array.reshape((self.size, array.shape[0] // self.size) + array.shape[1:])
        return self.gather(self.scatter_sum(pieces, 0), 0).reshape(array.shape)


class Links:
    def __init__(self, rows, cols):
        cores = 2 if rows % 2 == 0 else 1
        near = 1
        while cols % (near * 2) == 0 and near * near * 8 <= cols * 2:
            near *= 2
        self.core = Group(rows, cols, "row", 1, cores)
        self.x = Group(rows, cols, "row", cores, rows // cores)
        self.y = Group(rows, cols, "col", 1, near)
        self.z = Group(rows, cols, "col", near, cols // near)

    def row_total(self, array):
        pieces = array.reshape((self.core.size, array.shape[0] // self.core.size, array.shape[1]))
        part = self.x.total(self.core.scatter_sum(pieces, 0))
        return self.core.gather(part, 0).reshape(array.shape)

    def col_scatter(self, array):
        size = array.shape[0] // (self.z.size * self.y.size)
        pieces = array.reshape(self.z.size, self.y.size, size, array.shape[1])
        return self.z.scatter_sum(self.y.scatter_sum(pieces, 1), 0)

    def col_gather(self, array):
        whole = self.y.gather(self.z.gather(array, 0), 1)
        return whole.reshape(-1, array.shape[-1])


def place_kernel(count, map_ref, loads_ref, blocks_ref, out_ref):
    here = pl.program_id(0)
    out_ref[...] = loads_ref[...]
    for child in range(map_ref.shape[0]):
        source = map_ref[child, here]

        @pl.when(source < count)
        def _():
            out_ref[...] -= blocks_ref[child, source]


def place(loads, blocks, slots, part, parts):
    children, count, size, width = blocks.shape
    owned = slots.shape[1]
    return pl.pallas_call(
        lambda *refs: place_kernel(count, *refs),
        grid_spec=pltpu.PrefetchScalarGridSpec(
            num_scalar_prefetch=1,
            grid=(owned,),
            in_specs=[
                pl.BlockSpec((size, width), lambda i, slots: (i, part)),
                pl.BlockSpec((children, count, size, width), lambda i, slots: (0, 0, 0, 0)),
            ],
            out_specs=pl.BlockSpec((size, width), lambda i, slots: (i, 0)),
        ),
        out_shape=jax.ShapeDtypeStruct((owned * size, width), jnp.float32),
        compiler_params=pltpu.CompilerParams(vmem_limit_bytes=40 * 2**20),
    )(slots, loads, blocks)


def take_kernel(count, ids_ref, held_ref, out_ref):
    source = ids_ref[pl.program_id(0)]
    inside = jnp.logical_and(source >= 0, source < count)

    @pl.when(inside)
    def _():
        out_ref[...] = held_ref[...]

    @pl.when(jnp.logical_not(inside))
    def _():
        out_ref[...] = jnp.zeros_like(out_ref)


def take(held, ids):
    rows, width = held.shape
    count = rows // BLOCK
    wanted = ids.shape[0]
    return pl.pallas_call(
        lambda *refs: take_kernel(count, *refs),
        grid_spec=pltpu.PrefetchScalarGridSpec(
            num_scalar_prefetch=1,
            grid=(wanted,),
            in_specs=[
                pl.BlockSpec(
                    (BLOCK, width), lambda i, ids: (jnp.clip(ids[i], 0, count - 1), 0)
                ),
            ],
            out_specs=pl.BlockSpec((BLOCK, width), lambda i, ids: (i, 0)),
        ),
        out_shape=jax.ShapeDtypeStruct((wanted * BLOCK, width), jnp.float32),
    )(ids, held)


def general(rows, cols, *arguments):
    inverses = arguments[0:4]
    couplings = arguments[4:8]
    inverse_root = arguments[8]
    sources = arguments[9:13]
    loads_root = arguments[13]
    target_blocks = arguments[14]
    links = Links(rows, cols)
    columns = loads_root.shape[1]
    parts, width = 1, columns
    children, count = target_blocks.shape
    per_row = couplings[0].shape[0] // BLOCK
    owned = loads_root.shape[0] // BLOCK
    held = inverse_root.shape[0] // BLOCK

    owned_ids = lax.axis_index("row") * owned + jnp.arange(owned, dtype=jnp.int32)
    same = target_blocks[:, :, None] == owned_ids[None, None, :]
    numbers = jnp.arange(count, dtype=jnp.int32)[None, :, None]
    slots = jnp.min(jnp.where(same, numbers, count), axis=1)
    mine = lax.dynamic_slice_in_dim(target_blocks, lax.axis_index("row") * per_row, per_row, 1)
    wanted = (mine - lax.axis_index("col") * held).reshape(-1)

    answers = []
    for part in range(parts):
        span = slice(part * width, (part + 1) * width)
        forward = [
            links.row_total(product(weight, source[:, span]))
            for weight, source in zip(inverses, sources)
        ]
        partial_value = jnp.concatenate(
            [product(weight, solved) for weight, solved in zip(couplings, forward)]
        )
        summed = links.col_scatter(partial_value)
        spread = links.core.gather(links.x.gather(links.col_gather(summed), 0), 1)
        blocks = spread.reshape(rows, children, per_row, BLOCK, width)
        blocks = blocks.transpose(1, 0, 2, 3, 4).reshape(children, count, BLOCK, width)
        shifted = place(loads_root, blocks, slots, part, parts)
        solved_root = links.row_total(product(inverse_root, shifted))
        picked = links.col_gather(links.col_scatter(take(solved_root, wanted)))
        picked = picked.reshape(children, per_row * BLOCK, width)
        finals = []
        for child in range(4):
            correction = links.row_total(transposed(couplings[child], picked[child]))
            final = transposed(inverses[child], forward[child] - correction)
            finals.append(links.col_scatter(final))
        answers.append(finals + [solved_root])
    return tuple(jnp.concatenate(list(pieces), axis=1) for pieces in zip(*answers))


def split(value):
    high = value.astype(jnp.bfloat16)
    return high, (value - high.astype(jnp.float32)).astype(jnp.bfloat16)


def dot(first, second, flip=False):
    dims = (((0 if flip else 1,), (0,)), ((), ()))

    def one(a, b):
        return lax.dot_general(a, b, dims, preferred_element_type=jnp.float32)

    return one(first[0], second[0]) + (one(first[0], second[1]) + one(first[1], second[0]))


class Sequence:
    def __init__(self, me):
        self.me = me
        self.last = me

    def __call__(self, kernel, inputs, outputs, scratch=(), limit=24):
        whole = pl.BlockSpec(memory_space=pltpu.VMEM)
        count = len(inputs)
        results = pl.pallas_call(
            lambda *refs: kernel(*refs[: count + 1], *refs[count + 2 :]),
            in_specs=[pl.BlockSpec(memory_space=pltpu.SMEM)]
            + [whole] * count
            + [pl.BlockSpec(memory_space=pl.ANY)],
            out_specs=[whole] * len(outputs),
            out_shape=list(outputs),
            scratch_shapes=list(scratch),
            cost_estimate=COST,
            compiler_params=pltpu.CompilerParams(vmem_limit_bytes=limit * 2**20),
        )(self.me, *inputs, self.last)
        self.last = results[0]
        return results

    def hold(self, array):
        result = pl.pallas_call(
            lambda held, last, out: None,
            in_specs=[pl.BlockSpec(memory_space=pl.ANY)] * 2,
            out_specs=pl.BlockSpec(memory_space=pl.ANY),
            out_shape=shape(*array.shape),
            input_output_aliases={0: 0},
            cost_estimate=COST,
        )(array, self.last)
        self.last = result
        return result

    def merge(self, inputs, signs=None):
        signs = signs or (1,) * len(inputs)

        def kernel(me, *refs):
            refs[-1][...] = total([ref[...] for ref in refs[:-1]], signs)

        return self(kernel, inputs, [shape(*inputs[0].shape)])[0]

    def merge_split(self, inputs):
        count = inputs[0].shape[0]

        def kernel(me, *refs):
            sources, outs = refs[: len(inputs)], refs[len(inputs) :]
            for place in range(count):
                outs[place][...] = total([ref[place] for ref in sources], (1,) * len(inputs))

        return self(kernel, inputs, [shape(*inputs[0].shape[1:])] * count)

    def stack(self, inputs):
        def kernel(me, *refs):
            for place, ref in enumerate(refs[:-1]):
                refs[-1][place] = ref[...]

        return self(kernel, inputs, [shape(len(inputs), *inputs[0].shape)])[0]

    def join(self, inputs):
        rows = [a.shape[0] for a in inputs]

        def kernel(me, *refs):
            start = 0
            for ref, count in zip(refs[:-1], rows):
                refs[-1][start : start + count] = ref[...]
                start += count

        return self(kernel, inputs, [shape(sum(rows), *inputs[0].shape[1:])])[0]


def total(values, signs):
    result = values[0]
    for value, sign in zip(values[1:], signs[1:]):
        result = result + value if sign > 0 else result - value
    return result


def shape(*extent):
    return jax.ShapeDtypeStruct(extent, jnp.float32)


def part_of(half, part, width):
    parts = 2
    return pl.ds(pl.multiple_of((half * parts + part) * width, width), width)


def forward_kernel(parts, me, *refs):
    count = (len(refs) - 2 * len(parts)) // 2
    outs = refs[2 * count :]
    width = outs[0].shape[1]
    start = 0
    for weight, loads in zip(refs[:count], refs[count : 2 * count]):
        rows = weight.shape[0]
        pieces = [
            loads[:, part_of(half, part, width)] for part in parts for half in (me[0], 1 - me[0])
        ]
        value = dot(split(weight[...]), split(jnp.concatenate(pieces, axis=1)))
        for place, out in enumerate(outs):
            out[start : start + rows] = value[:, place * width : (place + 1) * width]
        start += rows


def couple_kernel(me, *refs):
    y, z = me[1], me[2]
    keep, send = refs[-2:]
    count = keep.shape[0]
    for child in range(count):
        weight, (own, other, start) = refs[child], refs[count + child]
        rows = weight.shape[1]
        span = slice(start, start + rows)
        held = jnp.concatenate([own[span], other[span]], axis=1)
        value = dot(split(weight[...]), split(held))
        place = child

        @pl.when(y == 0)
        def _():
            keep[place] = value[:BLOCK]
            send[place] = value[BLOCK:]

        @pl.when(y != 0)
        def _():
            keep[place] = value[BLOCK:]
            send[place] = value[:BLOCK]


def base_kernel(me, weight, mine, theirs, last, out, high, low):
    @pl.when(pl.program_id(0) == 0)
    def _():
        high[...], low[...] = split(jnp.concatenate([mine[...], theirs[...]], axis=1))

    out[...] = dot(split(weight[...]), (high[...], low[...]))


def base(sequence, part, piece, width, weight, loads):
    rows, depth = weight.shape[0] // 2, weight.shape[1]
    steps = 4
    tile = rows // steps
    parts = 2
    result = pl.pallas_call(
        base_kernel,
        grid_spec=pltpu.PrefetchScalarGridSpec(
            num_scalar_prefetch=1,
            grid=(steps,),
            in_specs=[
                pl.BlockSpec((tile, depth), lambda i, me: (piece * steps + i, 0)),
                pl.BlockSpec((depth, width), lambda i, me: (0, me[0] * parts + part)),
                pl.BlockSpec((depth, width), lambda i, me: (0, (1 - me[0]) * parts + part)),
                pl.BlockSpec(memory_space=pl.ANY),
            ],
            out_specs=pl.BlockSpec((tile, 2 * width), lambda i, me: (i, 0)),
            scratch_shapes=[pltpu.VMEM((depth, 2 * width), jnp.bfloat16)] * 2,
        ),
        out_shape=shape(rows, 2 * width),
        cost_estimate=COST,
        compiler_params=pltpu.CompilerParams(vmem_limit_bytes=40 * 2**20),
    )(sequence.me, weight, loads, loads, sequence.last)
    sequence.last = result
    return result


def root_kernel(list_ref, left, right, upper, lower, *refs):
    sources, (own, other_up, other_low, moved) = refs[:-5], refs[-4:]
    step = pl.program_id(0)
    width = own.shape[1]
    rows = own.shape[0]

    @pl.when(step == 0)
    def _():
        for start, ref, other in ((0, upper, other_up), (rows // 2, lower, other_low)):
            own[start : start + rows // 2] = ref[:, :width]
            other[...] = ref[:, width:]

    @pl.when(2 * step < list_ref[3, 0])
    def _():
        for entry in range(2):
            span = slice(entry * BLOCK, (entry + 1) * BLOCK)
            which = list_ref[1, 2 * step + entry]
            place = list_ref[2, 2 * step + entry]

            @pl.when(which < 0)
            def _():
                moved[span] = jnp.zeros((BLOCK, 2 * width), jnp.float32)

            for number, source in enumerate(sources):

                @pl.when(which == number)
                def _():
                    if number < 2:
                        moved[span] = source[place]
                    else:
                        moved[span, :width] = source[place, :, width:]
                        moved[span, width:] = source[place, :, :width]

        held = split(moved[...])
        tile = rows // 4
        for start in range(0, rows, tile):
            span = slice(start, start + tile)
            weight = split(jnp.concatenate([left[span], right[span]], axis=1))
            value = dot(weight, held)
            own[span] -= value[:, :width]
            other = other_up if start < rows // 2 else other_low
            there = start % (rows // 2)
            other[there : there + tile] -= value[:, width:]


def root(sequence, listed, weight, starts, sources):
    rows = weight.shape[0]
    width = starts[0].shape[1] // 2
    whole = pl.BlockSpec(memory_space=pltpu.VMEM)
    results = pl.pallas_call(
        root_kernel,
        grid_spec=pltpu.PrefetchScalarGridSpec(
            num_scalar_prefetch=1,
            grid=(listed.shape[1] // 2,),
            in_specs=[
                pl.BlockSpec((rows, BLOCK), lambda i, listed: (0, listed[0, 2 * i])),
                pl.BlockSpec((rows, BLOCK), lambda i, listed: (0, listed[0, 2 * i + 1])),
            ]
            + [whole] * (2 + len(sources))
            + [pl.BlockSpec(memory_space=pl.ANY)],
            out_specs=[whole] * 3,
            scratch_shapes=[pltpu.VMEM((2 * BLOCK, 2 * width), jnp.float32)],
        ),
        out_shape=[shape(rows, width)] + [shape(rows // 2, width)] * 2,
        cost_estimate=COST,
        compiler_params=pltpu.CompilerParams(vmem_limit_bytes=40 * 2**20),
    )(listed, weight, weight, *starts, *sources, sequence.last)
    sequence.last = results[0]
    return results


def pick_kernel(me, own, other, keep, send):
    y, z = me[1], me[2]
    count = own.shape[0] // BLOCK
    width = own.shape[1]
    children = keep.shape[0]
    for out, block in ((send, 1 - y), (keep, y)):
        for child in range(children):
            place = child
            source = me[3 + 2 * child + block]
            inside = jnp.logical_and(source >= 0, source < count)

            @pl.when(inside)
            def _():
                span = pl.ds(pl.multiple_of(source * BLOCK, BLOCK), BLOCK)
                out[place, :, :width] = own[span]
                out[place, :, width:] = other[span]

            @pl.when(jnp.logical_not(inside))
            def _():
                out[place] = jnp.zeros((BLOCK, 2 * width), jnp.float32)


def correct_kernel(pair, me, first, second, near, far, own, other, rows_ref):
    y, z = me[1], me[2]
    width = own.shape[1]
    children = near.shape[0]
    start = 0
    for child, weight in zip(pair, (first, second)):
        rows = weight.shape[1]
        rows_ref[pl.ds(pl.multiple_of(y * BLOCK, BLOCK), BLOCK)] = near[child]
        rows_ref[pl.ds(pl.multiple_of((1 - y) * BLOCK, BLOCK), BLOCK)] = far[child]
        value = dot(split(weight[...]), split(rows_ref[...]), True)
        own[start : start + rows] = value[:, :width]
        other[start : start + rows] = value[:, width:]
        start += rows


def final_kernel(me, first, second, own, other, *refs):
    outs, whole = refs[:-1], refs[-1]
    y, z = me[1], me[2]
    count = outs[0].shape[0]
    width = own.shape[1]
    start, place = 0, 0
    for weight, (keep, send) in ((first, outs[:2]), (second, outs[-2:])):
        rows, columns = weight.shape
        size = columns // (2 * count)
        span = slice(start, start + rows)
        held = jnp.concatenate([own[span], other[span]], axis=1)
        value = dot(split(weight[...]), split(held), True)
        whole[:columns, pl.ds(pl.multiple_of(me[0] * width, width), width)] = value[:, :width]
        whole[:columns, pl.ds(pl.multiple_of((1 - me[0]) * width, width), width)] = value[:, width:]
        for out, side in ((send, 1 - y), (keep, y)):
            for owner in range(count):
                taken = pl.ds(pl.multiple_of((2 * owner + side) * size, 8), size)
                out[jnp.bitwise_xor(owner, z), place : place + size] = whole[taken]
        start += rows
        place += size if len(outs) == 2 else 0


def join_add_kernel(me, base_ref, upper, lower, out):
    rows = upper.shape[0]
    out[:rows] = base_ref[:rows] + upper[...]
    out[rows:] = base_ref[rows:] + lower[...]


def halve_kernel(me, keep, arrived, send, held):
    for place in range(keep.shape[0]):
        out = send if place % 2 else held
        out[place // 2] = keep[place] + arrived[place]


def finish_kernel(terms, me, *refs):
    held = iter(refs[:-2])
    outs = refs[-2:]
    rows = outs[0].shape[0]
    parts = len(terms)
    width = outs[0].shape[1] // (2 * parts)
    for part, counts in enumerate(terms):
        values = [total([next(held)[...] for _ in range(count)], (1,) * count) for count in counts]
        if len(values) == 1:
            values = [values[0][:rows], values[0][rows:]]
        for out, value in zip(outs, values):
            for half in range(2):
                start = (half * parts + part) * width
                out[:, start : start + width] = value[:, half * width : (half + 1) * width]


def whole_kernel(me, *refs):
    out = refs[-1]
    width = refs[0].shape[1]
    for part in range(2):
        out[:, part_of(me[0], part, width)] = refs[2 * part][...]
        out[:, part_of(1 - me[0], part, width)] = refs[2 * part + 1][...]


def fast(rows, cols, *arguments):
    inverses = arguments[0:4]
    couplings = arguments[4:8]
    inverse_root = arguments[8]
    sources = arguments[9:13]
    loads_root = arguments[13]
    target_blocks = arguments[14]
    links = Links(rows, cols)
    core, x, y, z = links.core, links.x, links.y, links.z
    width = loads_root.shape[1] // 4
    children, count = target_blocks.shape
    per_row = count // rows
    owned = loads_root.shape[0] // BLOCK
    held = inverse_root.shape[0] // BLOCK
    row = lax.axis_index("row")
    pairs = ((0, 3), (1, 2))

    def send(array, group, step=1):
        return lax.ppermute(array, AXES, group.pairs[step - 1])

    mine = lax.dynamic_slice_in_dim(target_blocks, row * per_row, per_row, 1)
    wanted = (mine - lax.axis_index("col") * held).reshape(-1)
    me = jnp.concatenate([jnp.stack([core.place, y.place, z.place]).astype(jnp.int32), wanted])

    child = jnp.arange(children, dtype=jnp.int32)[:, None] + jnp.zeros((1, count), jnp.int32)
    block = jnp.arange(count, dtype=jnp.int32)[None, :] + jnp.zeros((children, 1), jnp.int32)
    from_row = block // per_row
    away_x = jnp.where(from_row // 2 == x.place, 0, 1)
    away_core = jnp.where(from_row % 2 == core.place, 0, 1)
    away_y = jnp.where(block % per_row == y.place, 0, 1)
    local_block = target_blocks - row * owned
    inside = ((local_block >= 0) & (local_block < owned)).reshape(-1)
    rank = jnp.cumsum(inside.astype(jnp.int32)) - 1
    entries = jnp.arange(inside.shape[0], dtype=jnp.int32)
    chosen = inside[None, :] & (rank[None, :] == entries[:, None])
    table = (local_block, away_core * 2 + away_x + 1, away_y * children + child)
    held_rows = jnp.sum(jnp.where(chosen[None], jnp.stack(table).reshape(3, 1, -1), 0), axis=2)
    found = jnp.sum(inside.astype(jnp.int32))
    last = jnp.sum(jnp.where(entries == found - 1, held_rows[0], 0))
    listed = jnp.stack(
        [
            jnp.where(entries < found, held_rows[0], last),
            held_rows[1] - 1,
            held_rows[2],
            jnp.zeros_like(entries) + found,
        ]
    )

    run = Sequence(me)
    parts = range(2)
    state = [dict() for _ in parts]

    def forward_start(pair, chosen):
        weights = [inverses[k] for k in pair]
        loads = [sources[k] for k in pair]
        n = sum(weight.shape[0] for weight in weights)
        outs = run(
            functools.partial(forward_kernel, chosen),
            weights + loads,
            [shape(n, width)] * (2 * len(chosen)),
            limit=56,
        )
        return [(own, send(other, core)) for own, other in zip(outs[::2], outs[1::2])]

    def forward_cross(own, arrived):
        own = run.merge([own, arrived])
        return own, send(own, x)

    def forward_end(own, arrived):
        own = run.merge([own, arrived])
        return own, send(own, core)

    def couple(part, arrays):
        flat = [a for own, other, _ in arrays for a in (own, other)]
        firsts = [start for _, _, start in arrays]

        def kernel(me, *refs):
            held = refs[children : 3 * children]
            triples = [(held[2 * k], held[2 * k + 1], firsts[k]) for k in range(children)]
            couple_kernel(me, *refs[:children], *triples, *refs[3 * children :])

        piece = shape(z.size, BLOCK, 2 * width)
        keep, sent = run(kernel, list(couplings) + flat, [piece] * 2, limit=40)
        state[part]["keep"], state[part]["arrived"] = keep, send(sent, y)

    def exchange(array, mask):
        flip = mask * y.size
        listed = [(r * cols + c, r * cols + (c ^ flip)) for r in range(rows) for c in range(cols)]
        return lax.ppermute(array, AXES, listed)

    def sum_y(part):
        value = run.merge([state[part]["keep"], state[part]["arrived"]])
        state[part]["terms"] = [value, exchange(value, 1)]

    def sum_z(part):
        value = run.merge(state[part]["terms"])
        state[part]["terms"] = [value, exchange(value, 2)]

    def gather_z(part):
        near = run.merge(state[part]["terms"])
        state[part]["near"], state[part]["far"] = near, send(near, y)

    def gather_y(part):
        near = run.join([state[part]["near"], state[part]["far"]])
        state[part]["blocks"] = [near, send(near, x), send(near, core)]

    def hold_far(part):
        near, far, near_there = state[part]["blocks"]
        far = run.hold(far)
        state[part]["blocks"] = [near, far, near_there, send(far, core)]

    def solve_root(part):
        own, upper, lower = root(run, listed, inverse_root, [state[part]["base"][0], state[part]["base"][1]], state[part]["blocks"])
        state[part]["root"] = own, send(upper, core), send(lower, core)

    def cross_root(part):
        own = run(join_add_kernel, list(state[part]["root"]), [shape(*state[part]["root"][0].shape)])[0]
        state[part]["root"] = own, send(own, x)

    def end_root(part):
        own = run.merge(list(state[part]["root"]))
        state[part]["root"] = own, send(own, core)

    def pick_root(part):
        piece = shape(children, BLOCK, 2 * width)
        keep, sent = run(pick_kernel, list(state[part]["root"]), [piece] * 2)
        state[part]["keep"], state[part]["arrived"] = keep, send(sent, y)

    def correct(part, group):
        pair = pairs[group]
        weights = [couplings[k] for k in pair]
        own, other = run(
            functools.partial(correct_kernel, pair),
            weights + [state[part]["near"], state[part]["far"]],
            [shape(sum(weight.shape[1] for weight in weights), width)] * 2,
            [pltpu.VMEM((per_row * BLOCK, 2 * width), jnp.float32)],
        )
        state[part][group] = own, send(other, core)

    def correct_cross(part, group):
        own = run.merge(list(state[part][group]))
        state[part][group] = own, send(own, x)

    def reduce(part, group):
        first = forward[part][group][0]
        own = run.merge([first] + list(state[part][group]), (1, -1, -1))
        state[part][group] = own, send(own, core)

    def split_of(part, group):
        return (2, 3) if (part, group) == (1, 1) else (group,)

    def final(part, group):
        weights = [inverses[k] for k in pairs[group]]
        sizes = [weight.shape[1] // cols for weight in weights]
        keys = split_of(part, group)
        sizes = sizes if len(keys) == 2 else [sum(sizes)]
        outs = run(
            final_kernel,
            weights + list(state[part][group]),
            [shape(z.size, size, 2 * width) for size in sizes for _ in range(2)],
            [pltpu.VMEM((max(weight.shape[1] for weight in weights), 2 * width), jnp.float32)],
            limit=40,
        )
        for key, keep, sent in zip(keys, outs[::2], outs[1::2]):
            state[part][key] = keep, send(sent, y)

    def final_y(part, group):
        keep, arrived = state[part][group]
        half = shape(z.size // 2, *keep.shape[1:])
        sent, held = run(halve_kernel, [keep, arrived], [half] * 2)
        state[part][group] = held, exchange(sent, 1)

    def final_z(part, group):
        held, away = run.merge_split(list(state[part][group]))
        state[part][group] = [held, exchange(away, 2)]

    def finish(group):
        sizes = [inverses[k].shape[1] // cols for k in pairs[group]]
        outs = [shape(size, 4 * width) for size in sizes]
        pieces = [[state[part][key] for key in split_of(part, group)] for part in parts]
        terms = [[len(piece) for piece in held] for held in pieces]
        inputs = [a for held in pieces for piece in held for a in piece]
        return run(functools.partial(finish_kernel, terms), inputs, outs)

    def final_last(part, group):
        state[part][group] = [run.merge(state[part][group])]

    def by_child(part):
        arrays = [None] * children
        for group, (a, b) in enumerate(pairs):
            own, other = forward[part][group]
            arrays[a] = own, other, 0
            arrays[b] = own, other, couplings[a].shape[1]
        return arrays

    forward = [[None, None] for _ in parts]

    def begin(group, chosen=(0, 1)):
        for part, piece in zip(chosen, forward_start(pairs[group], chosen)):
            forward[part][group] = piece

    def begin_part(part, group):
        begin(group, (part,))

    def cross(part, group):
        forward[part][group] = forward_cross(*forward[part][group])

    def end(part, group):
        forward[part][group] = forward_end(*forward[part][group])

    def couple_all(part):
        couple(part, by_child(part))

    def start_root(part, piece):
        held = base(run, part, piece, width, inverse_root, loads_root)
        state[part].setdefault("base", {})[piece] = held

    solved = [None] * 4

    def finish_pair(group):
        a, b = pairs[group]
        solved[a], solved[b] = finish(group)

    whole_root = []

    def whole():
        held = [a for part in parts for a in state[part]["root"]]
        whole_root.extend(run(whole_kernel, held, [shape(inverse_root.shape[0], 4 * width)]))

    named = dict(
        begin=begin,
        begin_part=begin_part,
        cross=cross,
        end=end,
        base=start_root,
        couple=couple_all,
        sum_y=sum_y,
        sum_z=sum_z,
        gather_z=gather_z,
        gather_y=gather_y,
        hold_far=hold_far,
        root=solve_root,
        cross_root=cross_root,
        end_root=end_root,
        pick=pick_root,
        pick_y=sum_y,
        pick_z=sum_z,
        pick_g=gather_z,
        whole=whole,
        correct=correct,
        correct_x=correct_cross,
        reduce=reduce,
        final=final,
        final_y=final_y,
        final_z=final_z,
        final_last=final_last,
        finish=finish_pair,
    )
    for name, *which in ORDER:
        named[name](*which)
    return tuple(solved) + (whole_root[0],)


def local(rows, cols, *arguments):
    links = Links(rows, cols)
    children, count = arguments[14].shape
    columns = arguments[13].shape[1]
    sizes = [arguments[k].shape[1] for k in range(4)]
    fits = (
        links.core.size == 2
        and links.x.size == 2
        and links.y.size == 2
        and children == 4
        and links.z.size == 4
        and count == 2 * rows
        and arguments[4].shape[0] == 2 * BLOCK
        and columns % 512 == 0
        and arguments[8].shape[0] % (16 * BLOCK) == 0
        and all(size % (cols * 16) == 0 for size in sizes)
        and all(arguments[k].shape[0] % 16 == 0 for k in range(4))
    )
    return (fast if fits else general)(rows, cols, *arguments)


def solution(mesh):
    rows, cols = mesh.shape["row"], mesh.shape["col"]
    matrices = [P("col", "row")] * 4 + [P("row", "col")] * 4 + [P("col", "row")]
    vectors = [P("row", None)] * 5
    return jax.shard_map(
        lambda *arguments: local(rows, cols, *arguments),
        mesh=mesh,
        in_specs=tuple(matrices + vectors + [P()]),
        out_specs=(P(AXES, None),) * 4 + (P("col", None),),
        check_vma=False,
    )
```

```python
import functools

import jax
import jax.numpy as jnp
from jax import lax
from jax.experimental import pallas as pl
from jax.experimental.pallas import tpu as pltpu
from jax.sharding import PartitionSpec as P

BLOCK = 128
AXES = ("row", "col")
COST = pl.CostEstimate(flops=1, bytes_accessed=1, transcendentals=0)

ORDER = (
    ("begin", 0),
    ("begin", 1),
    ("cross", 0, 0),
    ("cross", 0, 1),
    ("cross", 1, 0),
    ("cross", 1, 1),
    ("base", 0, 0),
    ("base", 0, 1),
    ("end", 0, 0),
    ("end", 0, 1),
    ("couple", 0),
    ("base", 1, 0),
    ("sum_y", 0),
    ("base", 1, 1),
    ("sum_z", 0),
    ("end", 1, 0),
    ("end", 1, 1),
    ("couple", 1),
    ("sum_y", 1),
    ("gather_z", 0),
    ("gather_y", 0),
    ("sum_z", 1),
    ("gather_z", 1),
    ("hold_far", 0),
    ("root", 0),
    ("cross_root", 0),
    ("gather_y", 1),
    ("end_root", 0),
    ("pick", 0),
    ("pick_y", 0),
    ("hold_far", 1),
    ("root", 1),
    ("pick_z", 0),
    ("cross_root", 1),
    ("pick_g", 0),
    ("end_root", 1),
    ("pick", 1),
    ("correct", 0, 0),
    ("correct", 0, 1),
    ("correct_x", 0, 0),
    ("correct_x", 0, 1),
    ("pick_y", 1),
    ("reduce", 0, 0),
    ("final", 0, 0),
    ("pick_z", 1),
    ("whole",),
    ("pick_g", 1),
    ("reduce", 0, 1),
    ("final", 0, 1),
    ("final_y", 0, 0),
    ("correct", 1, 0),
    ("correct", 1, 1),
    ("correct_x", 1, 0),
    ("correct_x", 1, 1),
    ("final_z", 0, 0),
    ("reduce", 1, 0),
    ("final", 1, 0),
    ("final_y", 0, 1),
    ("reduce", 1, 1),
    ("final", 1, 1),
    ("final_last", 0, 0),
    ("final_z", 0, 1),
    ("final_y", 1, 0),
    ("final_last", 0, 1),
    ("final_y", 1, 2),
    ("final_y", 1, 3),
    ("final_z", 1, 0),
    ("final_z", 1, 2),
    ("final_last", 1, 0),
    ("final_z", 1, 3),
    ("finish", 0),
    ("finish", 1),
)


def product(matrix, vector):
    return jnp.dot(
        matrix, vector, precision=lax.Precision.HIGH, preferred_element_type=jnp.float32
    )


def transposed(matrix, vector):
    return lax.dot_general(
        matrix,
        vector,
        (((0,), (0,)), ((), ())),
        precision=lax.Precision.HIGH,
        preferred_element_type=jnp.float32,
    )


def pick(array, index, axis):
    return lax.dynamic_index_in_dim(array, index, axis, keepdims=False)


class Group:
    def __init__(self, rows, cols, axis, stride, size):
        self.size = size
        self.place = lax.rem(lax.axis_index(axis) // stride, size)
        self.pairs = []
        for step in range(1, size):
            listed = []
            for r in range(rows):
                for c in range(cols):
                    old = r if axis == "row" else c
                    digit = old // stride % size
                    new = old + ((digit + step) % size - digit) * stride
                    there = (new, c) if axis == "row" else (r, new)
                    listed.append((r * cols + c, there[0] * cols + there[1]))
            self.pairs.append(listed)

    def scatter_sum(self, array, axis):
        total = pick(array, self.place, axis)
        for step in range(1, self.size):
            sent = pick(array, lax.rem(self.place + step, self.size), axis)
            total = total + lax.ppermute(sent, AXES, self.pairs[step - 1])
        return total

    def gather(self, array, axis):
        if self.size == 1:
            return jnp.expand_dims(array, axis)
        held = [array]
        for step in range(1, self.size):
            held.append(lax.ppermute(array, AXES, self.pairs[step - 1]))
        if self.size == 2:
            first = self.place == 0
            return jnp.stack(
                [jnp.where(first, held[0], held[1]), jnp.where(first, held[1], held[0])], axis
            )
        shape = array.shape[:axis] + (self.size,) + array.shape[axis:]
        out = jnp.zeros(shape, array.dtype)
        for step, value in enumerate(held):
            source = lax.rem(self.place + self.size - step, self.size)
            out = lax.dynamic_update_index_in_dim(out, value, source, axis)
        return out

    def total(self, array):
        if self.size == 2:
            return array + lax.ppermute(array, AXES, self.pairs[0])
        if self.size == 1:
            return array
        pieces = array.reshape((self.size, array.shape[0] // self.size) + array.shape[1:])
        return self.gather(self.scatter_sum(pieces, 0), 0).reshape(array.shape)


class Links:
    def __init__(self, rows, cols):
        cores = 2 if rows % 2 == 0 else 1
        near = 1
        while cols % (near * 2) == 0 and near * near * 8 <= cols * 2:
            near *= 2
        self.core = Group(rows, cols, "row", 1, cores)
        self.x = Group(rows, cols, "row", cores, rows // cores)
        self.y = Group(rows, cols, "col", 1, near)
        self.z = Group(rows, cols, "col", near, cols // near)

    def row_total(self, array):
        pieces = array.reshape((self.core.size, array.shape[0] // self.core.size, array.shape[1]))
        part = self.x.total(self.core.scatter_sum(pieces, 0))
        return self.core.gather(part, 0).reshape(array.shape)

    def col_scatter(self, array):
        size = array.shape[0] // (self.z.size * self.y.size)
        pieces = array.reshape(self.z.size, self.y.size, size, array.shape[1])
        return self.z.scatter_sum(self.y.scatter_sum(pieces, 1), 0)

    def col_gather(self, array):
        whole = self.y.gather(self.z.gather(array, 0), 1)
        return whole.reshape(-1, array.shape[-1])


def place_kernel(count, map_ref, loads_ref, blocks_ref, out_ref):
    here = pl.program_id(0)
    out_ref[...] = loads_ref[...]
    for child in range(map_ref.shape[0]):
        source = map_ref[child, here]

        @pl.when(source < count)
        def _():
            out_ref[...] -= blocks_ref[child, source]


def place(loads, blocks, slots, part, parts):
    children, count, size, width = blocks.shape
    owned = slots.shape[1]
    return pl.pallas_call(
        lambda *refs: place_kernel(count, *refs),
        grid_spec=pltpu.PrefetchScalarGridSpec(
            num_scalar_prefetch=1,
            grid=(owned,),
            in_specs=[
                pl.BlockSpec((size, width), lambda i, slots: (i, part)),
                pl.BlockSpec((children, count, size, width), lambda i, slots: (0, 0, 0, 0)),
            ],
            out_specs=pl.BlockSpec((size, width), lambda i, slots: (i, 0)),
        ),
        out_shape=jax.ShapeDtypeStruct((owned * size, width), jnp.float32),
        compiler_params=pltpu.CompilerParams(vmem_limit_bytes=40 * 2**20),
    )(slots, loads, blocks)


def take_kernel(count, ids_ref, held_ref, out_ref):
    source = ids_ref[pl.program_id(0)]
    inside = jnp.logical_and(source >= 0, source < count)

    @pl.when(inside)
    def _():
        out_ref[...] = held_ref[...]

    @pl.when(jnp.logical_not(inside))
    def _():
        out_ref[...] = jnp.zeros_like(out_ref)


def take(held, ids):
    rows, width = held.shape
    count = rows // BLOCK
    wanted = ids.shape[0]
    return pl.pallas_call(
        lambda *refs: take_kernel(count, *refs),
        grid_spec=pltpu.PrefetchScalarGridSpec(
            num_scalar_prefetch=1,
            grid=(wanted,),
            in_specs=[
                pl.BlockSpec(
                    (BLOCK, width), lambda i, ids: (jnp.clip(ids[i], 0, count - 1), 0)
                ),
            ],
            out_specs=pl.BlockSpec((BLOCK, width), lambda i, ids: (i, 0)),
        ),
        out_shape=jax.ShapeDtypeStruct((wanted * BLOCK, width), jnp.float32),
    )(ids, held)


def general(rows, cols, *arguments):
    inverses = arguments[0:4]
    couplings = arguments[4:8]
    inverse_root = arguments[8]
    sources = arguments[9:13]
    loads_root = arguments[13]
    target_blocks = arguments[14]
    links = Links(rows, cols)
    columns = loads_root.shape[1]
    parts, width = 1, columns
    children, count = target_blocks.shape
    per_row = couplings[0].shape[0] // BLOCK
    owned = loads_root.shape[0] // BLOCK
    held = inverse_root.shape[0] // BLOCK

    owned_ids = lax.axis_index("row") * owned + jnp.arange(owned, dtype=jnp.int32)
    same = target_blocks[:, :, None] == owned_ids[None, None, :]
    numbers = jnp.arange(count, dtype=jnp.int32)[None, :, None]
    slots = jnp.min(jnp.where(same, numbers, count), axis=1)
    mine = lax.dynamic_slice_in_dim(target_blocks, lax.axis_index("row") * per_row, per_row, 1)
    wanted = (mine - lax.axis_index("col") * held).reshape(-1)

    answers = []
    for part in range(parts):
        span = slice(part * width, (part + 1) * width)
        forward = [
            links.row_total(product(weight, source[:, span]))
            for weight, source in zip(inverses, sources)
        ]
        partial_value = jnp.concatenate(
            [product(weight, solved) for weight, solved in zip(couplings, forward)]
        )
        summed = links.col_scatter(partial_value)
        spread = links.core.gather(links.x.gather(links.col_gather(summed), 0), 1)
        blocks = spread.reshape(rows, children, per_row, BLOCK, width)
        blocks = blocks.transpose(1, 0, 2, 3, 4).reshape(children, count, BLOCK, width)
        shifted = place(loads_root, blocks, slots, part, parts)
        solved_root = links.row_total(product(inverse_root, shifted))
        picked = links.col_gather(links.col_scatter(take(solved_root, wanted)))
        picked = picked.reshape(children, per_row * BLOCK, width)
        finals = []
        for child in range(4):
            correction = links.row_total(transposed(couplings[child], picked[child]))
            final = transposed(inverses[child], forward[child] - correction)
            finals.append(links.col_scatter(final))
        answers.append(finals + [solved_root])
    return tuple(jnp.concatenate(list(pieces), axis=1) for pieces in zip(*answers))


def split(value):
    high = value.astype(jnp.bfloat16)
    return high, (value - high.astype(jnp.float32)).astype(jnp.bfloat16)


def dot(first, second, flip=False):
    dims = (((0 if flip else 1,), (0,)), ((), ()))

    def one(a, b):
        return lax.dot_general(a, b, dims, preferred_element_type=jnp.float32)

    return one(first[0], second[0]) + (one(first[0], second[1]) + one(first[1], second[0]))


class Sequence:
    def __init__(self, me):
        self.me = me
        self.last = me

    def __call__(self, kernel, inputs, outputs, scratch=(), limit=24):
        whole = pl.BlockSpec(memory_space=pltpu.VMEM)
        count = len(inputs)
        results = pl.pallas_call(
            lambda *refs: kernel(*refs[: count + 1], *refs[count + 2 :]),
            in_specs=[pl.BlockSpec(memory_space=pltpu.SMEM)]
            + [whole] * count
            + [pl.BlockSpec(memory_space=pl.ANY)],
            out_specs=[whole] * len(outputs),
            out_shape=list(outputs),
            scratch_shapes=list(scratch),
            cost_estimate=COST,
            compiler_params=pltpu.CompilerParams(vmem_limit_bytes=limit * 2**20),
        )(self.me, *inputs, self.last)
        self.last = results[0]
        return results

    def hold(self, array):
        result = pl.pallas_call(
            lambda held, last, out: None,
            in_specs=[pl.BlockSpec(memory_space=pl.ANY)] * 2,
            out_specs=pl.BlockSpec(memory_space=pl.ANY),
            out_shape=shape(*array.shape),
            input_output_aliases={0: 0},
            cost_estimate=COST,
        )(array, self.last)
        self.last = result
        return result

    def merge(self, inputs, signs=None):
        signs = signs or (1,) * len(inputs)

        def kernel(me, *refs):
            refs[-1][...] = total([ref[...] for ref in refs[:-1]], signs)

        return self(kernel, inputs, [shape(*inputs[0].shape)])[0]

    def merge_split(self, inputs):
        count = inputs[0].shape[0]

        def kernel(me, *refs):
            sources, outs = refs[: len(inputs)], refs[len(inputs) :]
            for place in range(count):
                outs[place][...] = total([ref[place] for ref in sources], (1,) * len(inputs))

        return self(kernel, inputs, [shape(*inputs[0].shape[1:])] * count)

    def stack(self, inputs):
        def kernel(me, *refs):
            for place, ref in enumerate(refs[:-1]):
                refs[-1][place] = ref[...]

        return self(kernel, inputs, [shape(len(inputs), *inputs[0].shape)])[0]

    def join(self, inputs):
        rows = [a.shape[0] for a in inputs]

        def kernel(me, *refs):
            start = 0
            for ref, count in zip(refs[:-1], rows):
                refs[-1][start : start + count] = ref[...]
                start += count

        return self(kernel, inputs, [shape(sum(rows), *inputs[0].shape[1:])])[0]


def total(values, signs):
    result = values[0]
    for value, sign in zip(values[1:], signs[1:]):
        result = result + value if sign > 0 else result - value
    return result


def shape(*extent):
    return jax.ShapeDtypeStruct(extent, jnp.float32)


def part_of(half, part, width):
    parts = 2
    return pl.ds(pl.multiple_of((half * parts + part) * width, width), width)


def forward_kernel(parts, me, *refs):
    count = (len(refs) - 2 * len(parts)) // 2
    outs = refs[2 * count :]
    width = outs[0].shape[1]
    start = 0
    for weight, loads in zip(refs[:count], refs[count : 2 * count]):
        rows = weight.shape[0]
        pieces = [
            loads[:, part_of(half, part, width)] for part in parts for half in (me[0], 1 - me[0])
        ]
        value = dot(split(weight[...]), split(jnp.concatenate(pieces, axis=1)))
        for place, out in enumerate(outs):
            out[start : start + rows] = value[:, place * width : (place + 1) * width]
        start += rows


def couple_kernel(me, *refs):
    y, z = me[1], me[2]
    keep, send = refs[-2:]
    count = keep.shape[0]
    for child in range(count):
        weight, (own, other, start) = refs[child], refs[count + child]
        rows = weight.shape[1]
        span = slice(start, start + rows)
        held = jnp.concatenate([own[span], other[span]], axis=1)
        value = dot(split(weight[...]), split(held))
        place = child

        @pl.when(y == 0)
        def _():
            keep[place] = value[:BLOCK]
            send[place] = value[BLOCK:]

        @pl.when(y != 0)
        def _():
            keep[place] = value[BLOCK:]
            send[place] = value[:BLOCK]


def base_kernel(me, weight, mine, theirs, last, out, high, low):
    @pl.when(pl.program_id(0) == 0)
    def _():
        high[...], low[...] = split(jnp.concatenate([mine[...], theirs[...]], axis=1))

    out[...] = dot(split(weight[...]), (high[...], low[...]))


def base(sequence, part, piece, width, weight, loads):
    rows, depth = weight.shape[0] // 2, weight.shape[1]
    steps = 4
    tile = rows // steps
    parts = 2
    result = pl.pallas_call(
        base_kernel,
        grid_spec=pltpu.PrefetchScalarGridSpec(
            num_scalar_prefetch=1,
            grid=(steps,),
            in_specs=[
                pl.BlockSpec((tile, depth), lambda i, me: (piece * steps + i, 0)),
                pl.BlockSpec((depth, width), lambda i, me: (0, me[0] * parts + part)),
                pl.BlockSpec((depth, width), lambda i, me: (0, (1 - me[0]) * parts + part)),
                pl.BlockSpec(memory_space=pl.ANY),
            ],
            out_specs=pl.BlockSpec((tile, 2 * width), lambda i, me: (i, 0)),
            scratch_shapes=[pltpu.VMEM((depth, 2 * width), jnp.bfloat16)] * 2,
        ),
        out_shape=shape(rows, 2 * width),
        cost_estimate=COST,
        compiler_params=pltpu.CompilerParams(vmem_limit_bytes=40 * 2**20),
    )(sequence.me, weight, loads, loads, sequence.last)
    sequence.last = result
    return result


def root_kernel(list_ref, left, right, upper, lower, *refs):
    sources, (own, other_up, other_low, moved) = refs[:-5], refs[-4:]
    step = pl.program_id(0)
    width = own.shape[1]
    rows = own.shape[0]

    @pl.when(step == 0)
    def _():
        for start, ref, other in ((0, upper, other_up), (rows // 2, lower, other_low)):
            own[start : start + rows // 2] = ref[:, :width]
            other[...] = ref[:, width:]

    @pl.when(2 * step < list_ref[3, 0])
    def _():
        for entry in range(2):
            span = slice(entry * BLOCK, (entry + 1) * BLOCK)
            which = list_ref[1, 2 * step + entry]
            place = list_ref[2, 2 * step + entry]

            @pl.when(which < 0)
            def _():
                moved[span] = jnp.zeros((BLOCK, 2 * width), jnp.float32)

            for number, source in enumerate(sources):

                @pl.when(which == number)
                def _():
                    if number < 2:
                        moved[span] = source[place]
                    else:
                        moved[span, :width] = source[place, :, width:]
                        moved[span, width:] = source[place, :, :width]

        held = split(moved[...])
        tile = rows // 4
        for start in range(0, rows, tile):
            span = slice(start, start + tile)
            weight = split(jnp.concatenate([left[span], right[span]], axis=1))
            value = dot(weight, held)
            own[span] -= value[:, :width]
            other = other_up if start < rows // 2 else other_low
            there = start % (rows // 2)
            other[there : there + tile] -= value[:, width:]


def root(sequence, listed, weight, starts, sources):
    rows = weight.shape[0]
    width = starts[0].shape[1] // 2
    whole = pl.BlockSpec(memory_space=pltpu.VMEM)
    results = pl.pallas_call(
        root_kernel,
        grid_spec=pltpu.PrefetchScalarGridSpec(
            num_scalar_prefetch=1,
            grid=(listed.shape[1] // 2,),
            in_specs=[
                pl.BlockSpec((rows, BLOCK), lambda i, listed: (0, listed[0, 2 * i])),
                pl.BlockSpec((rows, BLOCK), lambda i, listed: (0, listed[0, 2 * i + 1])),
            ]
            + [whole] * (2 + len(sources))
            + [pl.BlockSpec(memory_space=pl.ANY)],
            out_specs=[whole] * 3,
            scratch_shapes=[pltpu.VMEM((2 * BLOCK, 2 * width), jnp.float32)],
        ),
        out_shape=[shape(rows, width)] + [shape(rows // 2, width)] * 2,
        cost_estimate=COST,
        compiler_params=pltpu.CompilerParams(vmem_limit_bytes=40 * 2**20),
    )(listed, weight, weight, *starts, *sources, sequence.last)
    sequence.last = results[0]
    return results


def pick_kernel(me, own, other, keep, send):
    y, z = me[1], me[2]
    count = own.shape[0] // BLOCK
    width = own.shape[1]
    children = keep.shape[0]
    for out, block in ((send, 1 - y), (keep, y)):
        for child in range(children):
            place = child
            source = me[3 + 2 * child + block]
            inside = jnp.logical_and(source >= 0, source < count)

            @pl.when(inside)
            def _():
                span = pl.ds(pl.multiple_of(source * BLOCK, BLOCK), BLOCK)
                out[place, :, :width] = own[span]
                out[place, :, width:] = other[span]

            @pl.when(jnp.logical_not(inside))
            def _():
                out[place] = jnp.zeros((BLOCK, 2 * width), jnp.float32)


def correct_kernel(pair, me, first, second, near, far, own, other, rows_ref):
    y, z = me[1], me[2]
    width = own.shape[1]
    children = near.shape[0]
    start = 0
    for child, weight in zip(pair, (first, second)):
        rows = weight.shape[1]
        rows_ref[pl.ds(pl.multiple_of(y * BLOCK, BLOCK), BLOCK)] = near[child]
        rows_ref[pl.ds(pl.multiple_of((1 - y) * BLOCK, BLOCK), BLOCK)] = far[child]
        value = dot(split(weight[...]), split(rows_ref[...]), True)
        own[start : start + rows] = value[:, :width]
        other[start : start + rows] = value[:, width:]
        start += rows


def final_kernel(me, first, second, own, other, *refs):
    outs, whole = refs[:-1], refs[-1]
    y, z = me[1], me[2]
    count = outs[0].shape[0]
    width = own.shape[1]
    start, place = 0, 0
    for weight, (keep, send) in ((first, outs[:2]), (second, outs[-2:])):
        rows, columns = weight.shape
        size = columns // (2 * count)
        span = slice(start, start + rows)
        held = jnp.concatenate([own[span], other[span]], axis=1)
        value = dot(split(weight[...]), split(held), True)
        whole[:columns, pl.ds(pl.multiple_of(me[0] * width, width), width)] = value[:, :width]
        whole[:columns, pl.ds(pl.multiple_of((1 - me[0]) * width, width), width)] = value[:, width:]
        for out, side in ((send, 1 - y), (keep, y)):
            for owner in range(count):
                taken = pl.ds(pl.multiple_of((2 * owner + side) * size, 8), size)
                out[jnp.bitwise_xor(owner, z), place : place + size] = whole[taken]
        start += rows
        place += size if len(outs) == 2 else 0


def join_add_kernel(me, base_ref, upper, lower, out):
    rows = upper.shape[0]
    out[:rows] = base_ref[:rows] + upper[...]
    out[rows:] = base_ref[rows:] + lower[...]


def halve_kernel(me, keep, arrived, send, held):
    for place in range(keep.shape[0]):
        out = send if place % 2 else held
        out[place // 2] = keep[place] + arrived[place]


def finish_kernel(terms, me, *refs):
    held = iter(refs[:-2])
    outs = refs[-2:]
    rows = outs[0].shape[0]
    parts = len(terms)
    width = outs[0].shape[1] // (2 * parts)
    for part, counts in enumerate(terms):
        values = [total([next(held)[...] for _ in range(count)], (1,) * count) for count in counts]
        if len(values) == 1:
            values = [values[0][:rows], values[0][rows:]]
        for out, value in zip(outs, values):
            for half in range(2):
                start = (half * parts + part) * width
                out[:, start : start + width] = value[:, half * width : (half + 1) * width]


def whole_kernel(me, *refs):
    out = refs[-1]
    width = refs[0].shape[1]
    for part in range(2):
        out[:, part_of(me[0], part, width)] = refs[2 * part][...]
        out[:, part_of(1 - me[0], part, width)] = refs[2 * part + 1][...]


def fast(rows, cols, *arguments):
    inverses = arguments[0:4]
    couplings = arguments[4:8]
    inverse_root = arguments[8]
    sources = arguments[9:13]
    loads_root = arguments[13]
    target_blocks = arguments[14]
    links = Links(rows, cols)
    core, x, y, z = links.core, links.x, links.y, links.z
    width = loads_root.shape[1] // 4
    children, count = target_blocks.shape
    per_row = count // rows
    owned = loads_root.shape[0] // BLOCK
    held = inverse_root.shape[0] // BLOCK
    row = lax.axis_index("row")
    pairs = ((0, 3), (1, 2))

    def send(array, group, step=1):
        return lax.ppermute(array, AXES, group.pairs[step - 1])

    mine = lax.dynamic_slice_in_dim(target_blocks, row * per_row, per_row, 1)
    wanted = (mine - lax.axis_index("col") * held).reshape(-1)
    me = jnp.concatenate([jnp.stack([core.place, y.place, z.place]).astype(jnp.int32), wanted])

    child = jnp.arange(children, dtype=jnp.int32)[:, None] + jnp.zeros((1, count), jnp.int32)
    block = jnp.arange(count, dtype=jnp.int32)[None, :] + jnp.zeros((children, 1), jnp.int32)
    from_row = block // per_row
    away_x = jnp.where(from_row // 2 == x.place, 0, 1)
    away_core = jnp.where(from_row % 2 == core.place, 0, 1)
    away_y = jnp.where(block % per_row == y.place, 0, 1)
    local_block = target_blocks - row * owned
    inside = ((local_block >= 0) & (local_block < owned)).reshape(-1)
    rank = jnp.cumsum(inside.astype(jnp.int32)) - 1
    entries = jnp.arange(inside.shape[0], dtype=jnp.int32)
    chosen = inside[None, :] & (rank[None, :] == entries[:, None])
    table = (local_block, away_core * 2 + away_x + 1, away_y * children + child)
    held_rows = jnp.sum(jnp.where(chosen[None], jnp.stack(table).reshape(3, 1, -1), 0), axis=2)
    found = jnp.sum(inside.astype(jnp.int32))
    last = jnp.sum(jnp.where(entries == found - 1, held_rows[0], 0))
    listed = jnp.stack(
        [
            jnp.where(entries < found, held_rows[0], last),
            held_rows[1] - 1,
            held_rows[2],
            jnp.zeros_like(entries) + found,
        ]
    )

    run = Sequence(me)
    parts = range(2)
    state = [dict() for _ in parts]

    def forward_start(pair, chosen):
        weights = [inverses[k] for k in pair]
        loads = [sources[k] for k in pair]
        n = sum(weight.shape[0] for weight in weights)
        outs = run(
            functools.partial(forward_kernel, chosen),
            weights + loads,
            [shape(n, width)] * (2 * len(chosen)),
            limit=56,
        )
        return [(own, send(other, core)) for own, other in zip(outs[::2], outs[1::2])]

    def forward_cross(own, arrived):
        own = run.merge([own, arrived])
        return own, send(own, x)

    def forward_end(own, arrived):
        own = run.merge([own, arrived])
        return own, send(own, core)

    def couple(part, arrays):
        flat = [a for own, other, _ in arrays for a in (own, other)]
        firsts = [start for _, _, start in arrays]

        def kernel(me, *refs):
            held = refs[children : 3 * children]
            triples = [(held[2 * k], held[2 * k + 1], firsts[k]) for k in range(children)]
            couple_kernel(me, *refs[:children], *triples, *refs[3 * children :])

        piece = shape(z.size, BLOCK, 2 * width)
        keep, sent = run(kernel, list(couplings) + flat, [piece] * 2, limit=40)
        state[part]["keep"], state[part]["arrived"] = keep, send(sent, y)

    def exchange(array, mask):
        flip = mask * y.size
        listed = [(r * cols + c, r * cols + (c ^ flip)) for r in range(rows) for c in range(cols)]
        return lax.ppermute(array, AXES, listed)

    def sum_y(part):
        value = run.merge([state[part]["keep"], state[part]["arrived"]])
        state[part]["terms"] = [value, exchange(value, 1)]

    def sum_z(part):
        value = run.merge(state[part]["terms"])
        state[part]["terms"] = [value, exchange(value, 2)]

    def gather_z(part):
        near = run.merge(state[part]["terms"])
        state[part]["near"], state[part]["far"] = near, send(near, y)

    def gather_y(part):
        near = run.join([state[part]["near"], state[part]["far"]])
        state[part]["blocks"] = [near, send(near, x), send(near, core)]

    def hold_far(part):
        near, far, near_there = state[part]["blocks"]
        far = run.hold(far)
        state[part]["blocks"] = [near, far, near_there, send(far, core)]

    def solve_root(part):
        own, upper, lower = root(run, listed, inverse_root, [state[part]["base"][0], state[part]["base"][1]], state[part]["blocks"])
        state[part]["root"] = own, send(upper, core), send(lower, core)

    def cross_root(part):
        own = run(join_add_kernel, list(state[part]["root"]), [shape(*state[part]["root"][0].shape)])[0]
        state[part]["root"] = own, send(own, x)

    def end_root(part):
        own = run.merge(list(state[part]["root"]))
        state[part]["root"] = own, send(own, core)

    def pick_root(part):
        piece = shape(children, BLOCK, 2 * width)
        keep, sent = run(pick_kernel, list(state[part]["root"]), [piece] * 2)
        state[part]["keep"], state[part]["arrived"] = keep, send(sent, y)

    def correct(part, group):
        pair = pairs[group]
        weights = [couplings[k] for k in pair]
        own, other = run(
            functools.partial(correct_kernel, pair),
            weights + [state[part]["near"], state[part]["far"]],
            [shape(sum(weight.shape[1] for weight in weights), width)] * 2,
            [pltpu.VMEM((per_row * BLOCK, 2 * width), jnp.float32)],
        )
        state[part][group] = own, send(other, core)

    def correct_cross(part, group):
        own = run.merge(list(state[part][group]))
        state[part][group] = own, send(own, x)

    def reduce(part, group):
        first = forward[part][group][0]
        own = run.merge([first] + list(state[part][group]), (1, -1, -1))
        state[part][group] = own, send(own, core)

    def split_of(part, group):
        return (2, 3) if (part, group) == (1, 1) else (group,)

    def final(part, group):
        weights = [inverses[k] for k in pairs[group]]
        sizes = [weight.shape[1] // cols for weight in weights]
        keys = split_of(part, group)
        sizes = sizes if len(keys) == 2 else [sum(sizes)]
        outs = run(
            final_kernel,
            weights + list(state[part][group]),
            [shape(z.size, size, 2 * width) for size in sizes for _ in range(2)],
            [pltpu.VMEM((max(weight.shape[1] for weight in weights), 2 * width), jnp.float32)],
            limit=40,
        )
        for key, keep, sent in zip(keys, outs[::2], outs[1::2]):
            state[part][key] = keep, send(sent, y)

    def final_y(part, group):
        keep, arrived = state[part][group]
        half = shape(z.size // 2, *keep.shape[1:])
        sent, held = run(halve_kernel, [keep, arrived], [half] * 2)
        state[part][group] = held, exchange(sent, 1)

    def final_z(part, group):
        held, away = run.merge_split(list(state[part][group]))
        state[part][group] = [held, exchange(away, 2)]

    def finish(group):
        sizes = [inverses[k].shape[1] // cols for k in pairs[group]]
        outs = [shape(size, 4 * width) for size in sizes]
        pieces = [[state[part][key] for key in split_of(part, group)] for part in parts]
        terms = [[len(piece) for piece in held] for held in pieces]
        inputs = [a for held in pieces for piece in held for a in piece]
        return run(functools.partial(finish_kernel, terms), inputs, outs)

    def final_last(part, group):
        state[part][group] = [run.merge(state[part][group])]

    def by_child(part):
        arrays = [None] * children
        for group, (a, b) in enumerate(pairs):
            own, other = forward[part][group]
            arrays[a] = own, other, 0
            arrays[b] = own, other, couplings[a].shape[1]
        return arrays

    forward = [[None, None] for _ in parts]

    def begin(group, chosen=(0, 1)):
        for part, piece in zip(chosen, forward_start(pairs[group], chosen)):
            forward[part][group] = piece

    def begin_part(part, group):
        begin(group, (part,))

    def cross(part, group):
        forward[part][group] = forward_cross(*forward[part][group])

    def end(part, group):
        forward[part][group] = forward_end(*forward[part][group])

    def couple_all(part):
        couple(part, by_child(part))

    def start_root(part, piece):
        held = base(run, part, piece, width, inverse_root, loads_root)
        state[part].setdefault("base", {})[piece] = held

    solved = [None] * 4

    def finish_pair(group):
        a, b = pairs[group]
        solved[a], solved[b] = finish(group)

    whole_root = []

    def whole():
        held = [a for part in parts for a in state[part]["root"]]
        whole_root.extend(run(whole_kernel, held, [shape(inverse_root.shape[0], 4 * width)]))

    named = dict(
        begin=begin,
        begin_part=begin_part,
        cross=cross,
        end=end,
        base=start_root,
        couple=couple_all,
        sum_y=sum_y,
        sum_z=sum_z,
        gather_z=gather_z,
        gather_y=gather_y,
        hold_far=hold_far,
        root=solve_root,
        cross_root=cross_root,
        end_root=end_root,
        pick=pick_root,
        pick_y=sum_y,
        pick_z=sum_z,
        pick_g=gather_z,
        whole=whole,
        correct=correct,
        correct_x=correct_cross,
        reduce=reduce,
        final=final,
        final_y=final_y,
        final_z=final_z,
        final_last=final_last,
        finish=finish_pair,
    )
    for name, *which in ORDER:
        named[name](*which)
    return tuple(solved) + (whole_root[0],)


def local(rows, cols, *arguments):
    links = Links(rows, cols)
    children, count = arguments[14].shape
    columns = arguments[13].shape[1]
    sizes = [arguments[k].shape[1] for k in range(4)]
    fits = (
        links.core.size == 2
        and links.x.size == 2
        and links.y.size == 2
        and children == 4
        and links.z.size == 4
        and count == 2 * rows
        and arguments[4].shape[0] == 2 * BLOCK
        and columns % 512 == 0
        and arguments[8].shape[0] % (16 * BLOCK) == 0
        and all(size % (cols * 16) == 0 for size in sizes)
        and all(arguments[k].shape[0] % 16 == 0 for k in range(4))
    )
    return (fast if fits else general)(rows, cols, *arguments)


def solution(mesh):
    rows, cols = mesh.shape["row"], mesh.shape["col"]
    matrices = [P("col", "row")] * 4 + [P("row", "col")] * 4 + [P("col", "row")]
    vectors = [P("row", None)] * 5
    return jax.shard_map(
        lambda *arguments: local(rows, cols, *arguments),
        mesh=mesh,
        in_specs=tuple(matrices + vectors + [P()]),
        out_specs=(P(AXES, None),) * 4 + (P("col", None),),
        check_vma=False,
    )
```
